128 devices in a mesh: tp: 16 (over x, z_lo, core), dp: 8 (over y, z_hi).
Axes of the slice: x: 4, y: 4, z: 4 (z_hi: 2, z_lo: 2; z = z_hi * 2 + z_lo), core: 2. Of those that a mesh axis runs over, the one named last changes fastest.
Arguments:
- tokens: bfloat16 [8192, 8192], P(('dp', 'tp')), parts along dimension 0, may hold values from -8 to 8
- gain_attn: bfloat16 [8192], replicated, may hold values from 0.099609375 to 1.8984375
- w_query: bfloat16 [8192, 8192], P(None, 'tp')
- w_key: bfloat16 [8192, 1024], P(None, 'tp')
- w_value: bfloat16 [8192, 1024], P(None, 'tp'), may hold values from -0.0625 to 0.0625
- w_out: bfloat16 [8192, 8192], P('tp'), may hold values from -0.1875 to 0.1875
- gain_mlp: bfloat16 [8192], replicated, may hold values from 0.099609375 to 1.8984375
Outputs:
- stream: bfloat16 [8192, 8192], P(('dp', 'tp')), parts along dimension 0
- mlp_input: bfloat16 [8192, 8192], P(('dp', 'tp')), parts along dimension 0
The draws below stay inside these ranges and needn't reach their ends.
There are 8 independent parts, one for each index of `dp`. The reference program is written for one: setup_inputs(seed, part) draws one part's arguments, and reference() takes and returns one part's arrays. A program takes and returns all parts, laid end to end along the dimension named above; an argument that names none is the same for every part. Nothing has to cross between parts.
All inputs are finite; a program needn't handle non-finite values.
Results may differ from the reference program's by a relative error of at most 0.024.
Values may be sent and summed in bfloat16 or wider, within the bound.
A program may use at most 128 MiB of HBM per device.

```python
import math
import jax
import jax.numpy as jnp
from jax import lax

D = 8192
HEADS = 64
KVH = 8
HD = 128
TOK = 1024
N_TP = 16


def draw_tokens(key, part):
    key = jax.random.fold_in(key, 13)
    first_key, second_key, third_key = jax.random.split(key, 3)
    row_scale = jnp.exp(jax.random.uniform(first_key, (TOK, 1), jnp.float32, math.log(0.1), 0.0))
    col_scale = jnp.exp(jax.random.uniform(second_key, (1, D), jnp.float32, math.log(0.5), math.log(2.0)))
    entries = jnp.clip(jax.random.normal(third_key, (TOK, D), jnp.float32), -4.0, 4.0)
    return (entries * row_scale * col_scale).astype(jnp.bfloat16)


def draw_w_query(key, part):
    own_key = jax.random.fold_in(key, 11)
    weights = jax.random.normal(own_key, (D, HEADS * HD), jnp.float32) * D ** (-0.5)
    return weights.astype(jnp.bfloat16)


def draw_w_key(key, part):
    own_key = jax.random.fold_in(key, 12)
    weights = jax.random.normal(own_key, (D, KVH * HD), jnp.float32) * D ** (-0.5)
    return weights.astype(jnp.bfloat16)


def level_of(stream_key, shape, shards, low, top_value):
    level, own = 1.0, jax.random.fold_in(stream_key, 6)
    for dim, blocks in shards:
        heights = jnp.exp(jax.random.uniform(jax.random.fold_in(own, dim), (blocks,), jnp.float32, low / len(shards), top_value / len(shards)))
        level = level * jnp.repeat(heights, shape[dim] // blocks).reshape([-1 if axis == dim else 1 for axis in range(len(shape))])
    return level


def scatter_about(rng, shape, width, bound, shards=(), kind=jnp.bfloat16):
    loudness = level_of(rng, shape, shards, -0.22, 0.18) if shards else 1.0
    values = jax.random.normal(rng, shape, jnp.float32) * width * loudness
    return jnp.minimum(jnp.maximum(values, -bound), bound).astype(kind)


def setup_inputs(seed: int = 0, part: int = 0) -> dict:
    splits = jax.random.split(jax.random.key(seed), 8)
    own_keys = jax.random.split(jax.random.fold_in(splits[7], part), 8)
    return {
        "tokens": draw_tokens(jax.random.fold_in(jax.random.fold_in(splits[7], part), 71), part),
        "gain_attn": jnp.clip(1.0 + 0.18 * jax.random.normal(splits[1], (D,), jnp.float32), 0.099609375, 1.8984375).astype(jnp.bfloat16),
        "w_query": draw_w_query(jax.random.fold_in(splits[7], 71), part),
        "w_key": draw_w_key(jax.random.fold_in(splits[7], 71), part),
        "w_value": scatter_about(splits[4], (D, KVH * HD), D ** -0.5, 0.0625, ((1, 16),)),
        "w_out": scatter_about(splits[5], (HEADS * HD, D), (8 * HD) ** -0.5, 0.1875, ((0, 16),)),
        "gain_mlp": jnp.clip(1.0 + 0.18 * jax.random.normal(splits[6], (D,), jnp.float32), 0.099609375, 1.8984375).astype(jnp.bfloat16),
    }


def rms_scaled(rows_in, gain):
    as_float = rows_in.astype(jnp.float32)
    inv_rms = lax.rsqrt(lax.optimization_barrier(jnp.mean(as_float * as_float, axis=-1, keepdims=True)) + 1e-05)
    return as_float * inv_rms * gain.astype(jnp.float32)

def rotary(as_float, positions, col_start):
    row_count, col_count = as_float.shape
    paired = as_float.reshape(row_count, col_count // 2, 2)
    pair_index = (col_start // 2 + jnp.arange(col_count // 2, dtype=jnp.int32)) % (HD // 2)
    inverse = jnp.exp(pair_index.astype(jnp.float32) * (-2.0 * math.log(500000.0) / HD))
    angles = positions[:, None] * inverse[None, :]
    cos_part = jnp.cos(angles)
    sine_part = jnp.sin(angles)
    even_part = paired[..., 0]
    odd_part = paired[..., 1]
    turned = jnp.stack([even_part * cos_part - odd_part * sine_part, even_part * sine_part + odd_part * cos_part], axis=-1)
    return turned.reshape(row_count, col_count)

def attend(query_heads, key_heads, value_heads):
    row_count = query_heads.shape[0]
    scores = jnp.einsum('qhd,khd->hqk', query_heads.astype(jnp.float32), key_heads.astype(jnp.float32)) * HD ** (-0.5)
    visible = jnp.arange(row_count)[:, None] >= jnp.arange(row_count)[None, :]
    scores = jnp.where(visible[None, :, :], scores, -1e+30)
    row_top = lax.optimization_barrier(jnp.max(scores, axis=-1, keepdims=True))
    soft_weights = jnp.exp(scores - row_top)
    probs = (soft_weights / lax.optimization_barrier(jnp.sum(soft_weights, axis=-1, keepdims=True))).astype(jnp.bfloat16)
    context = jnp.einsum('hqk,khd->qhd', probs.astype(jnp.float32), value_heads.astype(jnp.float32))
    return context.astype(jnp.bfloat16).reshape(row_count, -1)

def reference(tokens, gain_attn, w_query, w_key, w_value, w_out, gain_mlp):
    row_count = tokens.shape[0]
    normed = rms_scaled(tokens, gain_attn).astype(jnp.bfloat16)
    positions = jnp.arange(row_count, dtype=jnp.int32).astype(jnp.float32)
    query_full = rotary(jnp.dot(normed, w_query, preferred_element_type=jnp.float32), positions, 0).astype(jnp.bfloat16)
    key_full = rotary(jnp.dot(normed, w_key, preferred_element_type=jnp.float32), positions, 0).astype(jnp.bfloat16)
    value_full = jnp.dot(normed, w_value, preferred_element_type=jnp.float32).astype(jnp.bfloat16)
    group_size = HEADS // KVH
    key_heads = jnp.repeat(key_full.reshape(row_count, KVH, HD), group_size, axis=1)
    value_heads = jnp.repeat(value_full.reshape(row_count, KVH, HD), group_size, axis=1)
    context = attend(query_full.reshape(row_count, HEADS, HD), key_heads, value_heads)
    local_cols = HEADS * HD // N_TP
    ctx_groups = context.reshape(row_count, N_TP, local_cols).transpose(1, 0, 2)
    out_groups = w_out.reshape(N_TP, local_cols, D)

    def add_group(summed, paired_in):
        part_term = jnp.dot(paired_in[0], paired_in[1], preferred_element_type=jnp.float32).astype(jnp.bfloat16)
        part_term = lax.optimization_barrier(part_term)
        return (summed + part_term.astype(jnp.float32), None)
    head_sum, ignored = lax.scan(add_group, jnp.zeros((row_count, D), jnp.float32), (ctx_groups, out_groups))
    stream = (tokens.astype(jnp.float32) + head_sum).astype(jnp.bfloat16)
    stream = lax.optimization_barrier(stream)
    mlp_input = rms_scaled(stream, gain_mlp).astype(jnp.bfloat16)
    return (stream, mlp_input)
```

```python
import math

import jax
import jax.numpy as jnp
import numpy as np
from jax import lax
from jax.experimental import pallas as pl
from jax.experimental.pallas import tpu as pltpu
from jax.sharding import PartitionSpec as P

MESH = pl.DeviceIdType.MESH
BF16 = jnp.bfloat16
F32 = jnp.float32
D = 8192
HD = 128
NX = 4
BLK = 256
PIECE = 2048
NQ = D // PIECE
HEADS = 4
WCH = 1024


def rotary_tables():
    inverse = np.exp(np.arange(HD // 2) * (-2.0 * math.log(500000.0) / HD))
    angles = np.arange(NX * BLK)[:, None] * inverse[None, :]
    cos = np.repeat(np.cos(angles), 2, axis=1).astype(np.float32)
    sin = np.repeat(np.sin(angles), 2, axis=1)
    sin[:, 0::2] *= -1.0
    return cos, sin.astype(np.float32)


def kernel(
    tok_hbm, gain_attn, wq_hbm, wk_hbm, wv_hbm, wo_hbm, gain_mlp, cos_hbm, sin_hbm,
    stream_hbm, mlp_hbm,
    xs, wq, wkv, wkst, wvst, wo, qb, kvl, kvr, ctx, ctxr, acc, cos, sin, bias, rz, rr, rx, tok,
    s_in, s_wst, s_send, s_xr, s_zr, s_sib, s_w, s_kvs, s_kvr, s_ctx, s_rsend, s_rz, s_rr, s_rx, s_out,
):
    tp, dp = lax.axis_index("tp"), lax.axis_index("dp")
    x, zl, c = tp // 4, (tp // 2) % 2, tp % 2
    y, zz = dp // 2, (dp % 2) * 2 + zl

    def device(x_to, z_to, c_to):
        return (x_to * 4 + (z_to % 2) * 2 + c_to, y * 2 + z_to // 2)

    right, left = device((x + 1) % 4, zz, c), device((x + 3) % 4, zz, c)
    above, below = device(x, (zz + 1) % 4, c), device(x, (zz + 3) % 4, c)
    across, sibling = device(x, (zz + 2) % 4, c), device(x, zz, 1 - c)
    b_own, b_right, b_far, b_left = x, (x + 1) % 4, (x + 2) % 4, (x + 3) % 4

    def remote(src, dst, send_sem, recv_sem, to):
        return pltpu.make_async_remote_copy(
            src_ref=src, dst_ref=dst, send_sem=send_sem, recv_sem=recv_sem,
            device_id=to, device_id_type=MESH,
        )

    def cols(q):
        return pl.ds(pl.multiple_of(q * PIECE, PIECE), PIECE)

    def rows(start, size):
        return pl.ds(pl.multiple_of(start, 32), size)

    tok_copy = pltpu.make_async_copy(tok_hbm, tok, s_in.at[0])
    tok_copy.start()
    barrier = pltpu.get_barrier_semaphore()
    for neighbour in (right, left, above, below, across, sibling):
        pl.semaphore_signal(barrier, inc=1, device_id=neighbour, device_id_type=MESH)

    def stage(k):
        part = pl.ds(k * WCH, WCH)
        return (
            pltpu.make_async_copy(wk_hbm.at[part], wkst.at[k % 2], s_wst.at[0, k % 2]),
            pltpu.make_async_copy(wv_hbm.at[part], wvst.at[k % 2], s_wst.at[1, k % 2]),
        )

    for k in range(2):
        for copy in stage(k):
            copy.start()
    in_copies = [
        pltpu.make_async_copy(wq_hbm, wq, s_in.at[1]),
        pltpu.make_async_copy(cos_hbm, cos, s_in.at[2]),
        pltpu.make_async_copy(sin_hbm, sin, s_in.at[3]),
        pltpu.make_async_copy(wo_hbm, wo.at[0], s_in.at[4]),
    ]
    for copy in in_copies:
        copy.start()

    tok_copy.wait()

    def norm_rows(i, carry):
        part = pl.ds(pl.multiple_of(i * 16, 16), 16)
        as_float = tok[part, :].astype(F32)
        inv = lax.rsqrt(jnp.mean(as_float * as_float, axis=-1, keepdims=True) + 1e-05)
        normed = as_float * inv * gain_attn[...].astype(F32)
        xs[x, pl.ds(pl.multiple_of(c * 64 + i * 16, 16), 16), :] = normed.astype(BF16)
        return carry

    lax.fori_loop(0, 4, norm_rows, 0)
    pl.semaphore_wait(barrier, 6)

    own_rows = rows(c * 64, 64)
    from_below = 192 - 64 * zl
    from_above = 128 + 64 * zl

    def send_x(b, q, way):
        ref = xs.at[b, own_rows, cols(q)]
        return remote(ref, ref, s_send.at[way, b], s_xr.at[b, q], (right, left)[way])

    def send_z(b, q, way):
        src = xs.at[b, rows(c * 64 + 32 * way, 32), cols(q)]
        at = (from_above, from_below)[way]
        dst = xs.at[b, rows(at + c * 32, 32), cols(q)]
        return remote(src, dst, s_send.at[2 + way, b], s_zr.at[way, b, q], (above, below)[way])

    def recv_z(b, q, way):
        at = (from_below, from_above)[way]
        ref = xs.at[b, rows(at + c * 32, 32), cols(q)]
        remote(ref, ref, s_send.at[2 + way, b], s_zr.at[way, b, q], sibling).wait_recv()

    def sib_ref(b, q, kind, core):
        if kind == 0:
            return xs.at[b, rows(core * 64, 64), cols(q)]
        at = (from_below, from_above)[kind - 1]
        return xs.at[b, rows(at + core * 32, 32), cols(q)]

    def send_sib(b, q, kind):
        ref = sib_ref(b, q, kind, c)
        remote(ref, ref, s_send.at[4 + kind, b], s_sib.at[kind, b, q], sibling).start()

    def recv_sib(b, q):
        for kind in range(3):
            ref = sib_ref(b, q, kind, 1 - c)
            remote(ref, ref, s_send.at[4 + kind, b], s_sib.at[kind, b, q], sibling).wait_recv()

    def spread(b, q):
        send_z(b, q, 0).start()
        send_z(b, q, 1).start()
        send_sib(b, q, 0)

    def start_own(q, carry):
        send_x(b_own, q, 0).start()
        send_x(b_own, q, 1).start()
        spread(b_own, q)
        return carry

    lax.fori_loop(0, NQ, start_own, 0)
    wo_send = remote(wo_hbm, wo.at[1], s_w.at[0], s_w.at[1], sibling)

    wkv_cols = pl.ds(pl.multiple_of(c * HD, HD), HD)
    for k in range(D // WCH):
        for copy in stage(k):
            copy.wait()
        joined = jnp.concatenate([wkst[k % 2], wvst[k % 2]], axis=1)
        wkv[pl.ds(k * WCH, WCH), wkv_cols] = joined
        if k + 2 < D // WCH:
            for copy in stage(k + 2):
                copy.start()
    wkv_send = remote(wkv.at[:, wkv_cols], wkv.at[:, wkv_cols], s_w.at[2], s_w.at[3], sibling)
    wkv_send.start()
    wo_send.start()

    def place(row):
        other = row >= 192
        inner = jnp.where(other, row - 192, row - 128)
        half = jnp.where(other, zl, 1 - zl)
        far = (1 - zl) * 128 + (inner // 32) * 64 + half * 32 + inner % 32
        return jnp.where(row < 128, zl * 128 + row, far)

    queries = place(lax.broadcasted_iota(jnp.int32, (BLK, BLK), 0))
    keys = place(lax.broadcasted_iota(jnp.int32, (BLK, BLK), 1))
    bias[...] = jnp.where(queries >= keys, 0.0, -1e30)
    acc[...] = jnp.zeros_like(acc)

    def qkv(a, b, q):
        held = xs[b, :, cols(q)]
        depth = cols(q)
        for n in range(2):
            part = pl.ds(n * 256, 256)
            acc[a, :, part] += jnp.dot(held, wq[depth, part], preferred_element_type=F32)
        acc[a, :, pl.ds(512, 256)] += jnp.dot(held, wkv[depth, :], preferred_element_type=F32)

    def table(ref, b):
        at = b * BLK
        far = at + (1 - zl) * 128
        parts = [ref[rows(at + zl * 128, 128), :]]
        for half in (1 - zl, zl):
            for core in range(2):
                parts.append(ref[rows(far + core * 64 + half * 32, 32), :])
        return jnp.concatenate(parts, axis=0)

    def kv_rows(b):
        return kvl.at[b, rows(c * 128, 128), :], kvr.at[b, rows(c * 128, 128), :]

    def kv_send(b):
        src, dst = kv_rows(b)
        return remote(src, dst, s_kvs.at[0, b], s_kvr.at[0, b], across)

    def kv_pass(b):
        ref = kv_rows(b)[1]
        return remote(ref, ref, s_kvs.at[1, b], s_kvr.at[1, b], sibling)

    def kv_wait(b):
        ref = kvr.at[b, rows((1 - c) * 128, 128), :]
        remote(ref, ref, s_kvs.at[1, b], s_kvr.at[1, b], sibling).wait_recv()

    def finish_qkv(a, b):
        cos_rows, sin_rows = table(cos, b), table(sin, b)
        lane = lax.broadcasted_iota(jnp.int32, (BLK, HD), 1)

        def turned(value):
            swapped = jnp.where(lane % 2 == 0, pltpu.roll(value, HD - 1, 1), pltpu.roll(value, 1, 1))
            return value * cos_rows + swapped * sin_rows

        first, second = acc[a, :, 512:640], acc[a, :, 640:768]
        key = jnp.where(lane < 64, first, pltpu.roll(second, 64, 1))
        value = jnp.where(lane < 64, pltpu.roll(first, 64, 1), second)
        kvl[b, :, 0:HD] = turned(key).astype(BF16)
        kvl[b, :, HD : 2 * HD] = value.astype(BF16)
        kv_send(b).start()
        scale = HD**-0.5 * math.log2(math.e)
        for h in range(HEADS):
            head = turned(acc[a, :, h * HD : (h + 1) * HD])
            qb[b, h] = (head * scale).astype(BF16)

    in_copies[0].wait()

    def first_loop(q, carry):
        for b, way in ((b_left, 0), (b_right, 1)):
            send_x(b, q, way).wait_recv()
            spread(b, q)

        @pl.when(q < 2)
        def _():
            send_x(b_left, q, 0).start()

        @pl.when(q >= 2)
        def _():
            send_x(b_right, q, 1).start()

        for way in range(2):
            recv_z(b_own, q, way)
            send_sib(b_own, q, 1 + way)
        recv_sib(b_own, q)

        @pl.when(q == 0)
        def _():
            remote(
                wkv.at[:, pl.ds(pl.multiple_of((1 - c) * HD, HD), HD)],
                wkv.at[:, pl.ds(pl.multiple_of((1 - c) * HD, HD), HD)],
                s_w.at[2], s_w.at[3], sibling,
            ).wait_recv()

        qkv(0, b_own, q)
        return carry

    lax.fori_loop(0, NQ, first_loop, 0)
    in_copies[1].wait()
    in_copies[2].wait()
    finish_qkv(0, b_own)
    acc[0] = jnp.zeros((BLK, 768), F32)

    def far_piece(q, way):
        send_x(b_far, q, way).wait_recv()
        spread(b_far, q)

    def second_loop(q, carry):
        for b in (b_left, b_right):
            for way in range(2):
                recv_z(b, q, way)
                send_sib(b, q, 1 + way)

        @pl.when(q == 2)
        def _():
            far_piece(0, 0)
            far_piece(2, 1)

        @pl.when(q == 3)
        def _():
            far_piece(1, 0)
            far_piece(3, 1)

        def both(a, inner):
            b = (x + 1 + 2 * a) % 4
            recv_sib(b, q)
            qkv(a, b, q)
            return inner

        lax.fori_loop(0, 2, both, 0)
        return carry

    lax.fori_loop(0, NQ, second_loop, 0)

    def finish_both(a, carry):
        finish_qkv(a, (x + 1 + 2 * a) % 4)
        return carry

    lax.fori_loop(0, 2, finish_both, 0)
    acc[0] = jnp.zeros((BLK, 768), F32)
    kv_send(b_own).wait_recv()
    kv_pass(b_own).start()

    def third_loop(i, carry):
        q = (i % 2) * 2 + i // 2
        for way in range(2):
            recv_z(b_far, q, way)
            send_sib(b_far, q, 1 + way)
        recv_sib(b_far, q)
        qkv(0, b_far, q)
        return carry

    lax.fori_loop(0, NQ, third_loop, 0)
    finish_qkv(0, b_far)

    for b in (b_right, b_left):
        kv_send(b).wait_recv()
        kv_pass(b).start()
    for b in (b_own, b_right, b_left):
        kv_wait(b)

    def scored(b, h, kb):
        q_rows = qb[b, h]
        key_in = jnp.concatenate([kvl[kb, 0:192, 0:HD], kvr[kb, 192:256, 0:HD]], axis=0)
        key_out = jnp.concatenate([kvr[kb, 0:192, 0:HD], kvl[kb, 192:256, 0:HD]], axis=0)
        dims = (((1,), (1,)), ((), ()))
        inside = lax.dot_general(q_rows[0:192], key_in, dims, preferred_element_type=F32)
        outside = lax.dot_general(q_rows[192:256], key_out, dims, preferred_element_type=F32)
        return jnp.concatenate([inside, outside], axis=0)

    def step(scores, kb, state):
        top, total, out = state
        new_top = jnp.maximum(top, jnp.max(scores, axis=-1, keepdims=True))
        weights = jnp.exp2(scores - new_top)
        fade = jnp.exp2(top - new_top)
        total = total * fade + jnp.sum(weights, axis=-1, keepdims=True)
        weights = weights.astype(BF16)
        val_in = jnp.concatenate([kvl[kb, 0:192, HD:], kvr[kb, 192:256, HD:]], axis=0)
        val_out = jnp.concatenate([kvr[kb, 0:192, HD:], kvl[kb, 192:256, HD:]], axis=0)
        inside = jnp.dot(weights[0:192], val_in, preferred_element_type=F32)
        outside = jnp.dot(weights[192:256], val_out, preferred_element_type=F32)
        return new_top, total, out * fade + jnp.concatenate([inside, outside], axis=0)

    def attend(b):
        for h in range(HEADS):
            start = (
                jnp.full((BLK, 1), -1e30, F32),
                jnp.zeros((BLK, 1), F32),
                jnp.zeros((BLK, HD), F32),
            )
            state = lax.fori_loop(0, b, lambda kb, s: step(scored(b, h, kb), kb, s), start)
            _, total, out = step(scored(b, h, b) + bias[...], b, state)
            out = (out / total).astype(BF16)
            at = pl.ds(h * HD, HD)
            for core in range(2):
                ctx[b, core, 0:64, at] = out[core * 64 : core * 64 + 64]
                ctx[b, core, 64:96, at] = out[128 + core * 32 : 160 + core * 32]
                ctx[b, core, 96:128, at] = out[192 + core * 32 : 224 + core * 32]
        ctx_send(b).start()

    def ctx_send(b):
        return remote(ctx.at[b, 1 - c], ctxr.at[b], s_ctx.at[0, b], s_ctx.at[1, b], sibling)

    def rs_z(b, q, way):
        at = (64 + 32 * zl, 96 - 32 * zl)[way]
        return remote(
            xs.at[b, rows(at, 32), cols(q)],
            rz.at[b, pl.ds(32 - 32 * way, 32), cols(q)],
            s_rsend.at[way, b], s_rz.at[way, b, q], (above, below)[way],
        )

    def rs_z_wait(b, q):
        for way in range(2):
            ref = rz.at[b, pl.ds(32 - 32 * way, 32), cols(q)]
            remote(ref, ref, s_rsend.at[way, b], s_rz.at[way, b, q], sibling).wait_recv()

    def project(b, q):
        def tile(n, carry):
            at = pl.ds(pl.multiple_of(q * PIECE + n * 512, 512), 512)
            total = jnp.dot(ctx[b, c], wo[0, :, at], preferred_element_type=F32)
            total += jnp.dot(ctxr[b], wo[1, :, at], preferred_element_type=F32)
            xs[b, 0:128, at] = total.astype(BF16)
            return carry

        lax.fori_loop(0, PIECE // 512, tile, 0)
        rs_z(b, q, 0).start()
        rs_z(b, q, 1).start()

    def drain(b, whole):
        half, quarter = xs.at[b, 0:64], xs.at[b, 0:32]
        for way in range(2):
            remote(quarter, quarter, s_send.at[2 + way, b], s_zr.at[way, b, 0], sibling).wait_send()
        for kind, ref in enumerate((half, quarter, quarter)):
            remote(ref, ref, s_send.at[4 + kind, b], s_sib.at[kind, b, 0], sibling).wait_send()
        for way in whole:
            remote(half, half, s_send.at[way, b], s_xr.at[b, 0], sibling).wait_send()

    def drain_half(b, way):
        ref = xs.at[b, 0:64, 0 : D // 2]
        remote(ref, ref, s_send.at[way, b], s_xr.at[b, 0], sibling).wait_send()

    def place_sum(b, q, relay):
        rs_z_wait(b, q)
        total = xs[b, 0:64, cols(q)].astype(F32) + rz[b, :, cols(q)].astype(F32)
        if relay:
            total += rr[:, cols(q)].astype(F32)
        xs[b, 0:64, cols(q)] = total.astype(BF16)

    def rs_relay(q, way):
        return remote(
            xs.at[b_far, 0:64, cols(q)], rr.at[:, cols(q)],
            s_rsend.at[2 + way, b_far], s_rr.at[q], (right, left)[way],
        )

    def rs_last(q, way):
        b = (b_right, b_left)[way]
        return remote(
            xs.at[b, 0:64, cols(q)], rx.at[way, :, cols(q)],
            s_rsend.at[2 + way, b], s_rx.at[way, q], (right, left)[way],
        )

    kv_send(b_far).wait_recv()
    kv_pass(b_far).start()
    kv_wait(b_far)
    attend(b_far)
    drain(b_far, ())
    in_copies[3].wait()
    remote(wo_hbm, wo.at[1], s_w.at[0], s_w.at[1], sibling).wait_recv()
    ctx_send(b_far).wait_recv()

    def far_project(i, carry):
        project(b_far, (i % 2) * 2 + i // 2)
        return carry

    lax.fori_loop(0, NQ, far_project, 0)

    def attend_both(a, carry):
        attend((x + 1 + 2 * a) % 4)
        place_sum(b_far, a, False)
        rs_relay(a, 0).start()
        place_sum(b_far, a + 2, False)
        rs_relay(a + 2, 1).start()
        return carry

    lax.fori_loop(0, 2, attend_both, 0)
    drain(b_right, ())
    drain_half(b_right, 1)
    drain(b_left, ())
    drain_half(b_left, 0)
    ctx_send(b_right).wait_recv()
    ctx_send(b_left).wait_recv()

    def project_both(q, carry):
        def one(a, inner):
            project((x + 1 + 2 * a) % 4, q)
            return inner

        return lax.fori_loop(0, 2, one, carry)

    lax.fori_loop(0, NQ, project_both, 0)
    attend(b_own)
    drain(b_own, (0, 1))
    ctx_send(b_own).wait_recv()

    def relay_wait(q):
        ref = rr.at[:, cols(q)]
        remote(ref, ref, s_rsend.at[2, b_far], s_rr.at[q], sibling).wait_recv()

    def own_project(q, carry):
        project(b_own, q)
        relay_wait(q)

        @pl.when(q < 2)
        def _():
            place_sum(b_right, q, True)
            place_sum(b_left, q, False)

        @pl.when(q >= 2)
        def _():
            place_sum(b_right, q, False)
            place_sum(b_left, q, True)

        rs_last(q, 0).start()
        rs_last(q, 1).start()
        return carry

    lax.fori_loop(0, NQ, own_project, 0)

    def last_sum(q, squares):
        rs_z_wait(b_own, q)
        for way in range(2):
            ref = rx.at[way, :, cols(q)]
            remote(ref, ref, s_rsend.at[2, b_own], s_rx.at[way, q], sibling).wait_recv()
        head_sum = xs[b_own, 0:64, cols(q)].astype(F32) + rz[b_own, :, cols(q)].astype(F32)
        head_sum += rx[0, :, cols(q)].astype(F32) + rx[1, :, cols(q)].astype(F32)
        stream = (tok[:, cols(q)].astype(F32) + head_sum).astype(BF16)
        tok[:, cols(q)] = stream
        pltpu.make_async_copy(tok.at[:, cols(q)], stream_hbm.at[:, cols(q)], s_out.at[q]).start()
        as_float = stream.astype(F32)
        return squares + jnp.sum(as_float * as_float, axis=-1, keepdims=True)

    squares = lax.fori_loop(0, NQ, last_sum, jnp.zeros((64, 1), F32))
    inv_rms = lax.rsqrt(squares * (1.0 / D) + 1e-05)

    def mlp_rows(q, carry):
        gain = gain_mlp[:, cols(q)].astype(F32)
        rr[:, cols(q)] = (tok[:, cols(q)].astype(F32) * inv_rms * gain).astype(BF16)
        pltpu.make_async_copy(rr.at[:, cols(q)], mlp_hbm.at[:, cols(q)], s_out.at[NQ + q]).start()
        return carry

    lax.fori_loop(0, NQ, mlp_rows, 0)

    for q in range(NQ):
        pltpu.make_async_copy(tok.at[:, cols(q)], stream_hbm.at[:, cols(q)], s_out.at[q]).wait()
        pltpu.make_async_copy(rr.at[:, cols(q)], mlp_hbm.at[:, cols(q)], s_out.at[NQ + q]).wait()
    wo_send.wait_send()
    wkv_send.wait_send()
    for b in range(NX):
        kv_send(b).wait_send()
        kv_pass(b).wait_send()
        ctx_send(b).wait_send()
        for way in range(2):
            ref = rz.at[b, 0:32]
            remote(ref, ref, s_rsend.at[way, b], s_rz.at[way, b, 0], sibling).wait_send()
    for way in range(2):
        ref = rr.at[:, 0 : D // 2]
        remote(ref, ref, s_rsend.at[2 + way, b_far], s_rr.at[0], sibling).wait_send()
        ref = rx.at[way]
        b = (b_right, b_left)[way]
        remote(ref, ref, s_rsend.at[2 + way, b], s_rx.at[way, 0], sibling).wait_send()


def sublayer(tokens, gain_attn, w_query, w_key, w_value, w_out, gain_mlp):
    cos, sin = rotary_tables()
    any_spec = pl.BlockSpec(memory_space=pl.ANY)
    vmem_spec = pl.BlockSpec(memory_space=pltpu.VMEM)
    dma = pltpu.SemaphoreType.DMA
    shape = jax.ShapeDtypeStruct((64, D), BF16)
    return pl.pallas_call(
        kernel,
        out_shape=(shape, shape),
        in_specs=[any_spec, vmem_spec] + [any_spec] * 4 + [vmem_spec] + [any_spec] * 2,
        out_specs=(any_spec, any_spec),
        scratch_shapes=[
            pltpu.VMEM((NX, BLK, D), BF16),
            pltpu.VMEM((D, 512), BF16),
            pltpu.VMEM((D, 256), BF16),
            pltpu.VMEM((2, WCH, 64), BF16),
            pltpu.VMEM((2, WCH, 64), BF16),
            pltpu.VMEM((2, 512, D), BF16),
            pltpu.VMEM((NX, HEADS, BLK, HD), BF16),
            pltpu.VMEM((NX, BLK, 256), BF16),
            pltpu.VMEM((NX, BLK, 256), BF16),
            pltpu.VMEM((NX, 2, 128, 512), BF16),
            pltpu.VMEM((NX, 128, 512), BF16),
            pltpu.VMEM((2, BLK, 768), F32),
            pltpu.VMEM((NX * BLK, HD), F32),
            pltpu.VMEM((NX * BLK, HD), F32),
            pltpu.VMEM((BLK, BLK), F32),
            pltpu.VMEM((NX, 64, D), BF16),
            pltpu.VMEM((64, D), BF16),
            pltpu.VMEM((2, 64, D), BF16),
            pltpu.VMEM((64, D), BF16),
            dma((5,)),
            dma((2, 2)),
            dma((7, NX)),
            dma((NX, NQ)),
            dma((2, NX, NQ)),
            dma((3, NX, NQ)),
            dma((4,)),
            dma((2, NX)),
            dma((2, NX)),
            dma((2, NX)),
            dma((4, NX)),
            dma((2, NX, NQ)),
            dma((NQ,)),
            dma((2, NQ)),
            dma((2 * NQ,)),
        ],
        compiler_params=pltpu.CompilerParams(
            collective_id=0, has_side_effects=True, vmem_limit_bytes=63 * 2**20
        ),
        cost_estimate=pl.CostEstimate(
            flops=24_000_000_000, bytes_accessed=24_000_000, transcendentals=4_000_000
        ),
    )(
        tokens, gain_attn.reshape(1, D), w_query, w_key, w_value, w_out, gain_mlp.reshape(1, D),
        jnp.asarray(cos), jnp.asarray(sin),
    )


def solution(mesh):
    placed = (
        P(("dp", "tp"), None),
        P(),
        P(None, "tp"),
        P(None, "tp"),
        P(None, "tp"),
        P("tp", None),
        P(),
    )
    return jax.shard_map(
        sublayer,
        mesh=mesh,
        in_specs=placed,
        out_specs=(P(("dp", "tp"), None), P(("dp", "tp"), None)),
        check_vma=False,
    )
```

```python
import math

import jax
import jax.numpy as jnp
import numpy as np
from jax import lax
from jax.experimental import pallas as pl
from jax.experimental.pallas import tpu as pltpu
from jax.sharding import PartitionSpec as P

MESH = pl.DeviceIdType.MESH
BF16 = jnp.bfloat16
F32 = jnp.float32
D = 8192
HD = 128
NX = 4
BLK = 256
PIECE = 2048
NQ = D // PIECE
HEADS = 4
THIRD = D - PIECE


def rotary_tables():
    inverse = np.exp(np.arange(HD // 2) * (-2.0 * math.log(500000.0) / HD))
    angles = np.arange(NX * BLK)[:, None] * inverse[None, :]
    cos = np.repeat(np.cos(angles), 2, axis=1).astype(np.float32)
    sin = np.repeat(np.sin(angles), 2, axis=1)
    sin[:, 0::2] *= -1.0
    return cos, sin.astype(np.float32)


def kernel(
    tok_hbm, gains, wq_hbm, wk_hbm, wv_hbm, wo_hbm, cos_hbm, sin_hbm, out_hbm,
    xs, wq, wkv, wo, qb, kvl, kvr, ctx, ctxr, acc, cos, sin, rz, rz0, rr, rr0, rx, rx0, tok,
    s_in, s_send, s_xr, s_xe, s_zr, s_sib, s_w, s_kvs, s_kvr, s_ctx, s_rsend, s_rz, s_rr, s_rx, s_out,
):
    tp, dp = lax.axis_index("tp"), lax.axis_index("dp")
    x, zl, c = tp // 4, (tp // 2) % 2, tp % 2
    y, zz = dp // 2, (dp % 2) * 2 + zl

    def device(x_to, z_to, c_to):
        return (x_to * 4 + (z_to % 2) * 2 + c_to, y * 2 + z_to // 2)

    right, left = device((x + 1) % 4, zz, c), device((x + 3) % 4, zz, c)
    above, below = device(x, (zz + 1) % 4, c), device(x, (zz + 3) % 4, c)
    across, sibling = device(x, (zz + 2) % 4, c), device(x, zz, 1 - c)
    b_own, b_right, b_far, b_left = x, (x + 1) % 4, (x + 2) % 4, (x + 3) % 4

    def remote(src, dst, send_sem, recv_sem, to):
        return pltpu.make_async_remote_copy(
            src_ref=src, dst_ref=dst, send_sem=send_sem, recv_sem=recv_sem,
            device_id=to, device_id_type=MESH,
        )

    def sent(ref, sem):
        remote(ref, ref, sem, s_w.at[0], sibling).wait_send()

    def landed(ref, sem):
        remote(ref, ref, s_w.at[0], sem, sibling).wait_recv()

    def cols(q):
        return pl.ds(pl.multiple_of(q * PIECE, PIECE), PIECE)

    def rows(start, size):
        return pl.ds(pl.multiple_of(start, 32), size)

    tok_copy = pltpu.make_async_copy(tok_hbm, tok, s_in.at[0])
    tok_copy.start()
    barrier = pltpu.get_barrier_semaphore()
    for neighbour in (right, left, above, below, across, sibling):
        pl.semaphore_signal(barrier, inc=1, device_id=neighbour, device_id_type=MESH)

    wk_rows, wv_rows = rows(c * HD, 64), rows(c * HD + 64, 64)
    in_copies = [
        pltpu.make_async_copy(wk_hbm, wkv.at[wk_rows], s_in.at[1]),
        pltpu.make_async_copy(wv_hbm, wkv.at[wv_rows], s_in.at[2]),
        pltpu.make_async_copy(wq_hbm, wq, s_in.at[3]),
        pltpu.make_async_copy(cos_hbm, cos, s_in.at[4]),
        pltpu.make_async_copy(sin_hbm, sin, s_in.at[5]),
        pltpu.make_async_copy(wo_hbm, wo.at[0], s_in.at[6]),
    ]
    for copy in in_copies:
        copy.start()

    tok_copy.wait()

    def norm_rows(i, carry):
        part = pl.ds(pl.multiple_of(i * 16, 16), 16)
        as_float = tok[part, :].astype(F32)
        inv = lax.rsqrt(jnp.mean(as_float * as_float, axis=-1, keepdims=True) + 1e-05)
        normed = as_float * inv * gains[...].astype(F32)
        xs[x, pl.ds(pl.multiple_of(c * 64 + i * 16, 16), 16), :] = normed.astype(BF16)
        return carry

    lax.fori_loop(0, 4, norm_rows, 0)
    pl.semaphore_wait(barrier, 6)

    from_below = 192 - 64 * zl
    from_above = 128 + 64 * zl
    x_ways = (right, left)

    def part_ref(b, q, kind, core):
        if kind == 0:
            return xs.at[b, rows(core * 64, 64), cols(q)]
        at = (from_below, from_above)[kind - 1]
        return xs.at[b, rows(at + core * 32, 32), cols(q)]

    def half_ref(b, q, way):
        return xs.at[b, rows(c * 64 + 32 * way, 32), cols(q)]

    def send_x(b, q, way):
        ref = part_ref(b, q, 0, c)
        remote(ref, ref, s_send.at[way, b], s_xr.at[way, b, q], x_ways[way]).start()

    def send_half(b, q, way):
        ref = half_ref(b, q, way)
        remote(ref, ref, s_send.at[way, b], s_xr.at[way, b, q], x_ways[way]).start()

    def send_extra(b, kind, way):
        ref = part_ref(b, 0, kind, c)
        remote(ref, ref, s_send.at[7 + way, b], s_xe.at[kind - 1, b], x_ways[way]).start()

    def send_z(b, q):
        for way in range(2):
            at = (from_above, from_below)[way]
            dst = xs.at[b, rows(at + c * 32, 32), cols(q)]
            to = (above, below)[way]
            remote(half_ref(b, q, way), dst, s_send.at[2 + way, b], s_zr.at[way, b, q], to).start()

    def send_sib(b, q, kind):
        ref = part_ref(b, q, kind, c)
        remote(ref, ref, s_send.at[4 + kind, b], s_sib.at[kind, b, q], sibling).start()

    def recv_sib(b, q):
        for kind in range(3):
            landed(part_ref(b, q, kind, 1 - c), s_sib.at[kind, b, q])

    def pass_z(b, q):
        for way in range(2):
            landed(part_ref(b, q, 1 + way, c), s_zr.at[way, b, q])
            send_sib(b, q, 1 + way)

    def start_own(q, carry):
        send_z(b_own, q)

        @pl.when(q > 0)
        def _():
            send_x(b_own, q, 0)
            send_x(b_own, q, 1)

        send_sib(b_own, q, 0)
        return carry

    lax.fori_loop(0, NQ, start_own, 0)
    in_copies[0].wait()
    in_copies[1].wait()
    wkv_sends = [
        remote(wkv.at[wk_rows], wkv.at[wk_rows], s_w.at[0], s_w.at[3], sibling),
        remote(wkv.at[wv_rows], wkv.at[wv_rows], s_w.at[1], s_w.at[4], sibling),
    ]
    wo_send = remote(wo_hbm, wo.at[1], s_w.at[2], s_w.at[5], sibling)
    for copy in wkv_sends:
        copy.start()
    wo_send.start()
    acc[...] = jnp.zeros_like(acc)
    transposed = (((1,), (1,)), ((), ()))

    def qkv(a, b, q):
        held = xs[b, :, cols(q)]
        for n in range(2):
            part = pl.ds(n * 256, 256)
            acc[a, :, part] += jnp.dot(held, wq[cols(q), part], preferred_element_type=F32)
        acc[a, :, pl.ds(512, 256)] += lax.dot_general(
            held, wkv[:, cols(q)], transposed, preferred_element_type=F32
        )

    def table(ref, b):
        at = b * BLK
        far = at + (1 - zl) * 128
        parts = [ref[rows(at + zl * 128, 128), :]]
        for half in (1 - zl, zl):
            for core in range(2):
                parts.append(ref[rows(far + core * 64 + half * 32, 32), :])
        return jnp.concatenate(parts, axis=0)

    def kv_send(b):
        return remote(kvl.at[b, c], kvr.at[b, c], s_kvs.at[0, b], s_kvr.at[0, b], across)

    def kv_pass(b):
        return remote(kvr.at[b, c], kvr.at[b, c], s_kvs.at[1, b], s_kvr.at[1, b], sibling)

    def kv_wait(b):
        landed(kvr.at[b, 1 - c], s_kvr.at[1, b])

    def finish_qkv(a, b):
        cos_rows, sin_rows = table(cos, b), table(sin, b)
        lane = lax.broadcasted_iota(jnp.int32, (BLK, HD), 1)

        def turned(value):
            swapped = jnp.where(lane % 2 == 0, pltpu.roll(value, HD - 1, 1), pltpu.roll(value, 1, 1))
            return value * cos_rows + swapped * sin_rows

        first, second = acc[a, :, 512:640], acc[a, :, 640:768]
        key = turned(jnp.where(lane < 64, first, pltpu.roll(second, 64, 1))).astype(BF16)
        value = jnp.where(lane < 64, pltpu.roll(first, 64, 1), second).T.astype(BF16)
        for half in range(2):
            kvl[b, half, 0:128] = key[half * 128 : half * 128 + 128]
            kvl[b, half, 128:256] = value[:, half * 128 : half * 128 + 128]
        kv_send(b).start()
        scale = HD**-0.5 * math.log2(math.e)
        for h in range(HEADS):
            head = (turned(acc[a, :, h * HD : (h + 1) * HD]) * scale).astype(BF16)
            qb[b, h * 192 : h * 192 + 192] = head[0:192]
            qb[b, 768 + h * 64 : 832 + h * 64] = head[192:256]

    in_copies[2].wait()

    def first_loop(q, carry):
        @pl.when(q > 0)
        def _():
            for b, way in ((b_left, 0), (b_right, 1)):
                landed(part_ref(b, q, 0, c), s_xr.at[way, b, q])
                send_z(b, q)
                send_half(b, q, way)
                send_sib(b, q, 0)

        pass_z(b_own, q)
        recv_sib(b_own, q)

        @pl.when(q == 0)
        def _():
            other = rows((1 - c) * HD, 64), rows((1 - c) * HD + 64, 64)
            landed(wkv.at[other[0]], s_w.at[3])
            landed(wkv.at[other[1]], s_w.at[4])

        qkv(2, b_own, q)
        return carry

    lax.fori_loop(0, NQ, first_loop, 0)
    for way in range(2):
        send_x(b_own, 0, way)
    for way in range(2):
        send_extra(b_own, 1 + way, 0)
        send_extra(b_own, 1 + way, 1)
    in_copies[3].wait()
    in_copies[4].wait()
    finish_qkv(2, b_own)
    acc[2] = jnp.zeros((BLK, 768), F32)

    def both(fn):
        def one(a, carry):
            fn(a, (x + 1 + 2 * a) % 4)
            return carry

        lax.fori_loop(0, 2, one, 0)

    def far_rows(q):
        for way in range(2):
            landed(half_ref(b_far, q, way), s_xr.at[way, b_far, q])

    def second_loop(i, carry):
        q = i + 1
        for b in (b_left, b_right):
            pass_z(b, q)

        def near(a, b):
            recv_sib(b, q)
            qkv(a, b, q)

        both(near)
        far_rows(q)
        send_z(b_far, q)
        send_sib(b_far, q, 0)
        return carry

    lax.fori_loop(0, NQ - 1, second_loop, 0)

    def near_first(kind):
        for b, way in ((b_left, 0), (b_right, 1)):
            landed(part_ref(b, 0, kind, c), s_xr.at[way, b, 0] if kind == 0 else s_xe.at[kind - 1, b])
            if kind == 0:
                send_half(b, 0, way)
            elif kind == way + 1:
                send_extra(b, kind, way)
            send_sib(b, 0, kind)

    def third_loop(i, carry):
        for kind in range(3):
            pl.when(i == kind)(lambda kind=kind: near_first(kind))
        pass_z(b_far, i + 1)
        recv_sib(b_far, i + 1)
        qkv(2, b_far, i + 1)
        return carry

    lax.fori_loop(0, NQ - 1, third_loop, 0)
    kv_send(b_own).wait_recv()
    kv_pass(b_own).start()

    def near_last(a, b):
        recv_sib(b, 0)
        qkv(a, b, 0)
        finish_qkv(a, b)

    both(near_last)
    far_rows(0)
    send_sib(b_far, 0, 0)
    for kind in (1, 2):
        landed(part_ref(b_far, 0, kind, c), s_xe.at[kind - 1, b_far])
        send_sib(b_far, 0, kind)
    recv_sib(b_far, 0)
    qkv(2, b_far, 0)
    finish_qkv(2, b_far)

    for b in (b_right, b_left):
        kv_send(b).wait_recv()
        kv_pass(b).start()
    for b in (b_own, b_right, b_left):
        kv_wait(b)

    def place(row):
        other = row >= 192
        inner = jnp.where(other, row - 192, row - 128)
        half = jnp.where(other, zl, 1 - zl)
        far = (1 - zl) * 128 + (inner // 32) * 64 + half * 32 + inner % 32
        return jnp.where(row < 128, zl * 128 + row, far)

    def attend_step(b, kb, state, masked):
        low = lax.broadcasted_iota(jnp.int32, (HD, HD), 1) < 64

        def joined(mine, theirs):
            key = jnp.concatenate([mine[kb, 0, 0:128], mine[kb, 1, 0:64], theirs[kb, 1, 64:128]], axis=0)
            half = jnp.where(low, mine[kb, 1, 128:256].astype(F32), theirs[kb, 1, 128:256].astype(F32))
            return key, jnp.concatenate([mine[kb, 0, 128:256], half.astype(BF16)], axis=1)

        inside, outside = joined(kvl, kvr), joined(kvr, kvl)
        after = []
        for j in range(4):
            key, value = outside if j == 3 else inside
            top, total, out = state[j]
            at = pl.ds(j * BLK, BLK)
            scores = lax.dot_general(key, qb[b, at], transposed, preferred_element_type=F32)
            if masked:
                column = lax.broadcasted_iota(jnp.int32, (1, BLK), 1)
                column = 192 + column % 64 if j == 3 else (column + j * BLK) % 192
                row = lax.broadcasted_iota(jnp.int32, (BLK, 1), 0)
                scores = jnp.where(place(row) <= place(column), scores, -1e30)
            new_top = jnp.maximum(top, jnp.max(scores, axis=0, keepdims=True))
            weights = jnp.exp2(scores - new_top)
            fade = jnp.exp2(top - new_top)
            total = total * fade + jnp.sum(weights, axis=0, keepdims=True)
            out = out * fade + jnp.dot(value, weights.astype(BF16), preferred_element_type=F32)
            after.append((new_top, total, out))
        return tuple(after)

    def attend(b, before_last=None):
        start = tuple(
            (jnp.full((1, BLK), -1e30, F32), jnp.zeros((1, BLK), F32), jnp.zeros((HD, BLK), F32))
            for _ in range(4)
        )
        state = lax.fori_loop(0, b, lambda kb, s: attend_step(b, kb, s, False), start)
        if before_last is not None:
            before_last()
        state = attend_step(b, b, state, True)
        out = [(value / total).T.astype(BF16) for _, total, value in state]
        inside, outside = jnp.concatenate(out[:3], axis=0), out[3]
        for h in range(HEADS):
            at = pl.ds(h * HD, HD)
            for core in range(2):
                first, second = h * 192 + core * 64, h * 192 + 128 + core * 32
                third = h * 64 + core * 32
                ctx[b, core, 0:64, at] = inside[first : first + 64]
                ctx[b, core, 64:96, at] = inside[second : second + 32]
                ctx[b, core, 96:128, at] = outside[third : third + 32]
        ctx_send(b).start()

    def ctx_send(b):
        return remote(ctx.at[b, 1 - c], ctxr.at[b], s_ctx.at[0, b], s_ctx.at[1, b], sibling)

    def third_cols(q):
        return pl.ds(pl.multiple_of((q - 1) * PIECE, PIECE), PIECE)

    def project(b, q):
        def tile(n, carry):
            at = pl.ds(pl.multiple_of(q * PIECE + n * 512, 512), 512)
            total = jnp.dot(ctx[b, c], wo[0, :, at], preferred_element_type=F32)
            total += jnp.dot(ctxr[b], wo[1, :, at], preferred_element_type=F32)
            xs[b, 0:128, at] = total.astype(BF16)
            return carry

        lax.fori_loop(0, PIECE // 512, tile, 0)

    def rs_z(b, q):
        for way in range(2):
            at = (64 + 32 * zl, 96 - 32 * zl)[way]
            place_in = pl.ds(32 - 32 * way, 32)
            dst = rz0.at[place_in] if isinstance(q, int) else rz.at[b, place_in, third_cols(q)]
            src = xs.at[b, rows(at, 32), cols(q)]
            to = (above, below)[way]
            remote(src, dst, s_rsend.at[way, b], s_rz.at[way, b, q], to).start()

    def drain(b, kind):
        quarter, third = xs.at[b, 0:32], xs.at[b, 0:32, 0:THIRD]
        for way in range(2):
            sent(quarter if kind == "own" else third, s_send.at[2 + way, b])
        for part, ref in enumerate((xs.at[b, 0:64], quarter, quarter)):
            sent(ref, s_send.at[4 + part, b])
        if kind == "own":
            for way in range(2):
                sent(xs.at[b, 0:64], s_send.at[way, b])
                sent(xs.at[b, 0:64, 0:PIECE], s_send.at[7 + way, b])
        elif kind in (0, 1):
            sent(quarter, s_send.at[kind, b])
            sent(xs.at[b, 0:32, 0:PIECE], s_send.at[7 + kind, b])

    def sum_z(b, q):
        for way in range(2):
            landed(rz.at[b, pl.ds(32 - 32 * way, 32), third_cols(q)], s_rz.at[way, b, q])
        return xs[b, 0:64, cols(q)].astype(F32) + rz[b, :, third_cols(q)].astype(F32)

    def relay(q, way):
        part = pl.ds(32 * way, 32)
        to = x_ways[way]
        src, dst = xs.at[b_far, part, cols(q)], rr.at[way, :, cols(q)]
        remote(src, dst, s_rsend.at[2 + way, b_far], s_rr.at[way, q], to).start()
        if isinstance(q, int):
            src = xs.at[b_far, pl.ds(64 + 32 * way, 32), cols(0)]
            remote(src, rr0.at[way], s_rsend.at[4 + way, b_far], s_rr.at[way, NQ], to).start()

    def far_sum(q):
        xs[b_far, 0:64, cols(q)] = sum_z(b_far, q).astype(BF16)
        relay(q, 0)
        relay(q, 1)

    def near_sum_first(way):
        b, to = (b_right, b_left)[way], x_ways[way]
        landed(rr.at[way, :, cols(0)], s_rr.at[way, 0])
        landed(rr0.at[way], s_rr.at[way, NQ])
        for at, term in ((32 * way, rr[way, :, cols(0)]), (64 + 32 * way, rr0[way])):
            total = xs[b, at : at + 32, cols(0)].astype(F32) + term.astype(F32)
            xs[b, at : at + 32, cols(0)] = total.astype(BF16)
        src = xs.at[b, 0:128, cols(0)]
        remote(src, rx0.at[way], s_rsend.at[4 + way, b], s_rx.at[way, 0], to).start()

    def near_sum(q, way):
        b, to = (b_right, b_left)[way], x_ways[way]
        landed(rr.at[way, :, cols(q)], s_rr.at[way, q])
        total = sum_z(b, q)
        term = rr[way, :, cols(q)].astype(F32)
        first, second = total[0:32], total[32:64]
        if way == 0:
            first = first + term
        else:
            second = second + term
        xs[b, 0:32, cols(q)] = first.astype(BF16)
        xs[b, 32:64, cols(q)] = second.astype(BF16)
        dst = rx.at[way, :, third_cols(q)]
        remote(xs.at[b, 0:64, cols(q)], dst, s_rsend.at[2 + way, b], s_rx.at[way, q], to).start()

    def far_kv():
        kv_send(b_far).wait_recv()
        kv_pass(b_far).start()
        kv_wait(b_far)

    attend(b_far, far_kv)
    drain(b_far, "far")
    in_copies[5].wait()
    landed(wo.at[1], s_w.at[5])
    ctx_send(b_far).wait_recv()
    project(b_far, 0)
    relay(0, 0)
    relay(0, 1)

    def far_project(i, carry):
        project(b_far, i + 1)
        rs_z(b_far, i + 1)
        return carry

    lax.fori_loop(0, NQ - 1, far_project, 0)
    drain(b_right, 1)
    drain(b_left, 0)

    def near_project(a, b):
        attend(b)

        def sums(q, carry):
            far_sum(q)
            return carry

        lax.fori_loop(1 + a, 2 + 2 * a, sums, 0)
        ctx_send(b).wait_recv()

        def piece(i, carry):
            q = (i + 1) % NQ
            project(b, q)

            @pl.when(q > 0)
            def _():
                rs_z(b, q)

            return carry

        lax.fori_loop(0, NQ, piece, 0)

    both(near_project)
    near_sum_first(0)
    near_sum_first(1)
    attend(b_own)
    drain(b_own, "own")
    ctx_send(b_own).wait_recv()

    def own_project(i, carry):
        q = (i + 1) % NQ
        project(b_own, q)

        @pl.when(q > 0)
        def _():
            rs_z(b_own, q)

        return carry

    lax.fori_loop(0, NQ, own_project, 0)

    def near_sums(i, carry):
        near_sum(i + 1, 0)
        near_sum(i + 1, 1)
        return carry

    lax.fori_loop(0, NQ - 1, near_sums, 0)

    landed(rx0.at[0], s_rx.at[0, 0])
    landed(rx0.at[1], s_rx.at[1, 0])
    total = xs[b_own, 0:128, cols(0)].astype(F32) + rx0[0].astype(F32) + rx0[1].astype(F32)
    xs[b_own, 0:128, cols(0)] = total.astype(BF16)
    rs_z(b_own, 0)

    def store(q, head_sum):
        tok[:, cols(q)] = (tok[:, cols(q)].astype(F32) + head_sum).astype(BF16)
        pltpu.make_async_copy(tok.at[:, cols(q)], out_hbm.at[:, cols(q)], s_out.at[q]).start()

    def last_sum(q):
        total = sum_z(b_own, q)
        for way in range(2):
            landed(rx.at[way, :, third_cols(q)], s_rx.at[way, q])
        total += rx[0, :, third_cols(q)].astype(F32) + rx[1, :, third_cols(q)].astype(F32)
        store(q, total)

    def last_two(i, carry):
        last_sum(i + 1)
        return carry

    lax.fori_loop(0, 2, last_two, 0)
    for way in range(2):
        landed(rz0.at[pl.ds(32 - 32 * way, 32)], s_rz.at[way, b_own, 0])
    store(0, xs[b_own, 0:64, cols(0)].astype(F32) + rz0[...].astype(F32))
    lax.fori_loop(2, 3, last_two, 0)

    for q in range(NQ):
        pltpu.make_async_copy(tok.at[:, cols(q)], out_hbm.at[:, cols(q)], s_out.at[q]).wait()
    for copy in (*wkv_sends, wo_send):
        copy.wait_send()
    for b in range(NX):
        kv_send(b).wait_send()
        kv_pass(b).wait_send()
        ctx_send(b).wait_send()
    for way in range(2):
        for b in (b_far, b_right, b_left):
            sent(xs.at[b, 0:32, 0:THIRD], s_rsend.at[way, b])
        sent(xs.at[b_own, 0:32], s_rsend.at[way, b_own])
        sent(xs.at[b_far, 0:32], s_rsend.at[2 + way, b_far])
        sent(xs.at[b_far, 0:32, 0:PIECE], s_rsend.at[4 + way, b_far])
        b = (b_right, b_left)[way]
        sent(xs.at[b, 0:64, 0:THIRD], s_rsend.at[2 + way, b])
        sent(xs.at[b, 0:128, 0:PIECE], s_rsend.at[4 + way, b])


def final_norm(stream_in, gain, stream_out, mlp_out):
    stream = stream_in[...]
    stream_out[...] = stream
    as_float = stream.astype(F32)
    inv = lax.rsqrt(jnp.mean(as_float * as_float, axis=-1, keepdims=True) + 1e-05)
    mlp_out[...] = (as_float * inv * gain[...].astype(F32)).astype(BF16)


def sublayer(tokens, gain_attn, w_query, w_key, w_value, w_out, gain_mlp):
    cos, sin = rotary_tables()
    gain_attn, gain_mlp = gain_attn.reshape(1, D), gain_mlp.reshape(1, D)
    any_spec = pl.BlockSpec(memory_space=pl.ANY)
    vmem_spec = pl.BlockSpec(memory_space=pltpu.VMEM)
    dma = pltpu.SemaphoreType.DMA
    shape = jax.ShapeDtypeStruct((64, D), BF16)
    stream = pl.pallas_call(
        kernel,
        out_shape=shape,
        in_specs=[any_spec, vmem_spec] + [any_spec] * 6,
        out_specs=any_spec,
        scratch_shapes=[
            pltpu.VMEM((NX, BLK, D), BF16),
            pltpu.VMEM((D, 512), BF16),
            pltpu.VMEM((256, D), BF16),
            pltpu.VMEM((2, 512, D), BF16),
            pltpu.VMEM((NX, HEADS * BLK, HD), BF16),
            pltpu.VMEM((NX, 2, 256, HD), BF16),
            pltpu.VMEM((NX, 2, 256, HD), BF16),
            pltpu.VMEM((NX, 2, 128, 512), BF16),
            pltpu.VMEM((NX, 128, 512), BF16),
            pltpu.VMEM((3, BLK, 768), F32),
            pltpu.VMEM((NX * BLK, HD), F32),
            pltpu.VMEM((NX * BLK, HD), F32),
            pltpu.VMEM((NX, 64, THIRD), BF16),
            pltpu.VMEM((64, PIECE), BF16),
            pltpu.VMEM((2, 32, D), BF16),
            pltpu.VMEM((2, 32, PIECE), BF16),
            pltpu.VMEM((2, 64, THIRD), BF16),
            pltpu.VMEM((2, 128, PIECE), BF16),
            pltpu.VMEM((64, D), BF16),
            dma((7,)),
            dma((9, NX)),
            dma((2, NX, NQ)),
            dma((2, NX)),
            dma((2, NX, NQ)),
            dma((3, NX, NQ)),
            dma((6,)),
            dma((2, NX)),
            dma((2, NX)),
            dma((2, NX)),
            dma((6, NX)),
            dma((2, NX, NQ)),
            dma((2, NQ + 1)),
            dma((2, NQ)),
            dma((NQ,)),
        ],
        compiler_params=pltpu.CompilerParams(
            collective_id=0, has_side_effects=True, vmem_limit_bytes=63 * 2**20
        ),
        cost_estimate=pl.CostEstimate(
            flops=24_000_000_000, bytes_accessed=24_000_000, transcendentals=4_000_000
        ),
    )(
        tokens, gain_attn, w_query, w_key.T, w_value.T, w_out, jnp.asarray(cos), jnp.asarray(sin),
    )
    block = pl.BlockSpec((16, D), lambda i: (i, 0))
    return pl.pallas_call(
        final_norm,
        grid=(4,),
        out_shape=(shape, shape),
        in_specs=[block, pl.BlockSpec((1, D), lambda i: (0, 0))],
        out_specs=(block, block),
        compiler_params=pltpu.CompilerParams(vmem_limit_bytes=8 * 2**20),
        cost_estimate=pl.CostEstimate(flops=3_000_000, bytes_accessed=3_000_000, transcendentals=64),
    )(stream, gain_mlp)


def solution(mesh):
    placed = (
        P(("dp", "tp"), None),
        P(),
        P(None, "tp"),
        P(None, "tp"),
        P(None, "tp"),
        P("tp", None),
        P(),
    )
    return jax.shard_map(
        sublayer,
        mesh=mesh,
        in_specs=placed,
        out_specs=(P(("dp", "tp"), None), P(("dp", "tp"), None)),
        check_vma=False,
    )
```

```python
import math

import jax
import jax.numpy as jnp
import numpy as np
from jax import lax
from jax.experimental import pallas as pl
from jax.experimental.pallas import tpu as pltpu
from jax.sharding import PartitionSpec as P

MESH = pl.DeviceIdType.MESH
BF16 = jnp.bfloat16
F32 = jnp.float32
D = 8192
HD = 128
NX = 4
BLK = 256
PIECE = 2048
NQ = D // PIECE
HEADS = 4
THIRD = D - PIECE
FIRST = 1280
REST = (D - FIRST) // 3
WO_PARTS = 8
NCH = 8
CHUNK = HEADS * BLK // NCH


def rotary_tables():
    inverse = np.exp(np.arange(HD // 2) * (-2.0 * math.log(500000.0) / HD))
    angles = np.arange(NX * BLK)[:, None] * inverse[None, :]
    cos = np.repeat(np.cos(angles), 2, axis=1).astype(np.float32)
    sin = np.repeat(np.sin(angles), 2, axis=1)
    sin[:, 0::2] *= -1.0
    return cos, sin.astype(np.float32)


def kernel(
    tok_hbm, gains, wq_hbm, wk_hbm, wv_hbm, wo_hbm, cos_hbm, sin_hbm, out_hbm,
    xs, wq, wkv, wo, qb, kvl, kvr, ctx, ctxr, acc, cos, sin, rz, rz0, rr, rr0, rx, rx0, tok,
    s_in, s_send, s_xr, s_xe, s_zr, s_sib, s_w, s_kvs, s_kvr, s_ctx, s_rsend, s_rz, s_rr, s_rx, s_out,
):
    tp, dp = lax.axis_index("tp"), lax.axis_index("dp")
    x, zl, c = tp // 4, (tp // 2) % 2, tp % 2
    y, zz = dp // 2, (dp % 2) * 2 + zl

    def device(x_to, z_to, c_to):
        return (x_to * 4 + (z_to % 2) * 2 + c_to, y * 2 + z_to // 2)

    right, left = device((x + 1) % 4, zz, c), device((x + 3) % 4, zz, c)
    above, below = device(x, (zz + 1) % 4, c), device(x, (zz + 3) % 4, c)
    across, sibling = device(x, (zz + 2) % 4, c), device(x, zz, 1 - c)
    b_own, b_right, b_far, b_left = x, (x + 1) % 4, (x + 2) % 4, (x + 3) % 4

    def remote(src, dst, send_sem, recv_sem, to):
        return pltpu.make_async_remote_copy(
            src_ref=src, dst_ref=dst, send_sem=send_sem, recv_sem=recv_sem,
            device_id=to, device_id_type=MESH,
        )

    def sent(ref, sem):
        remote(ref, ref, sem, s_w.at[0], sibling).wait_send()

    def landed(ref, sem):
        remote(ref, ref, s_w.at[0], sem, sibling).wait_recv()

    def cols(q):
        return pl.ds(pl.multiple_of(q * PIECE, PIECE), PIECE)

    def rows(start, size):
        return pl.ds(pl.multiple_of(start, 32), size)

    tok_copy = pltpu.make_async_copy(tok_hbm, tok, s_in.at[0])
    tok_copy.start()
    barrier = pltpu.get_barrier_semaphore()
    for neighbour in (right, left, above, below, across, sibling):
        pl.semaphore_signal(barrier, inc=1, device_id=neighbour, device_id_type=MESH)

    wk_rows, wv_rows = rows(c * HD, 64), rows(c * HD + 64, 64)
    in_copies = [
        pltpu.make_async_copy(wk_hbm, wkv.at[wk_rows], s_in.at[1]),
        pltpu.make_async_copy(wv_hbm, wkv.at[wv_rows], s_in.at[2]),
        pltpu.make_async_copy(wq_hbm, wq, s_in.at[3]),
        pltpu.make_async_copy(cos_hbm, cos, s_in.at[4]),
        pltpu.make_async_copy(sin_hbm, sin, s_in.at[5]),
        pltpu.make_async_copy(wo_hbm, wo.at[0], s_in.at[6]),
    ]
    for copy in in_copies:
        copy.start()

    tok_copy.wait()

    def norm_rows(i, carry):
        part = pl.ds(pl.multiple_of(i * 16, 16), 16)
        as_float = tok[part, :].astype(F32)
        inv = lax.rsqrt(jnp.mean(as_float * as_float, axis=-1, keepdims=True) + 1e-05)
        normed = as_float * inv * gains[...].astype(F32)
        xs[x, pl.ds(pl.multiple_of(c * 64 + i * 16, 16), 16), :] = normed.astype(BF16)
        return carry

    lax.fori_loop(0, 4, norm_rows, 0)
    pl.semaphore_wait(barrier, 6)

    from_below = 192 - 64 * zl
    from_above = 128 + 64 * zl
    x_ways = (right, left)

    def part_ref(b, q, kind, core):
        if kind == 0:
            return xs.at[b, rows(core * 64, 64), cols(q)]
        at = (from_below, from_above)[kind - 1]
        return xs.at[b, rows(at + core * 32, 32), cols(q)]

    def half_ref(b, q, way):
        return xs.at[b, rows(c * 64 + 32 * way, 32), cols(q)]

    def send_x(b, q, way):
        ref = part_ref(b, q, 0, c)
        remote(ref, ref, s_send.at[way, b], s_xr.at[way, b, q], x_ways[way]).start()

    def send_half(b, q, way):
        ref = half_ref(b, q, way)
        remote(ref, ref, s_send.at[way, b], s_xr.at[way, b, q], x_ways[way]).start()

    def send_extra(b, kind, way):
        ref = part_ref(b, 0, kind, c)
        remote(ref, ref, s_send.at[7 + way, b], s_xe.at[kind - 1, b], x_ways[way]).start()

    def send_z(b, q):
        for way in range(2):
            at = (from_above, from_below)[way]
            dst = xs.at[b, rows(at + c * 32, 32), cols(q)]
            to = (above, below)[way]
            remote(half_ref(b, q, way), dst, s_send.at[2 + way, b], s_zr.at[way, b, q], to).start()

    def send_sib(b, q, kind):
        ref = part_ref(b, q, kind, c)
        remote(ref, ref, s_send.at[4 + kind, b], s_sib.at[kind, b, q], sibling).start()

    def recv_sib(b, q):
        for kind in range(3):
            landed(part_ref(b, q, kind, 1 - c), s_sib.at[kind, b, q])

    def pass_z(b, q):
        for way in range(2):
            landed(part_ref(b, q, 1 + way, c), s_zr.at[way, b, q])
            send_sib(b, q, 1 + way)

    def start_own(q, carry):
        send_z(b_own, q)

        @pl.when(q > 0)
        def _():
            send_x(b_own, q, 0)
            send_x(b_own, q, 1)

        send_sib(b_own, q, 0)
        return carry

    lax.fori_loop(0, NQ, start_own, 0)
    in_copies[0].wait()
    in_copies[1].wait()
    wkv_sends = [
        remote(wkv.at[wk_rows], wkv.at[wk_rows], s_w.at[0], s_w.at[3], sibling),
        remote(wkv.at[wv_rows], wkv.at[wv_rows], s_w.at[1], s_w.at[4], sibling),
    ]
    for copy in wkv_sends:
        copy.start()

    def wo_part(k):
        part = rows(k * (512 // WO_PARTS), 512 // WO_PARTS)
        return remote(wo_hbm.at[part], wo.at[1, part], s_w.at[2], s_w.at[5], sibling)

    acc[...] = jnp.zeros_like(acc)
    transposed = (((1,), (1,)), ((), ()))

    def qkv_q(a, b, q):
        held = xs[b, :, cols(q)]
        for n in range(2):
            part = pl.ds(n * 256, 256)
            acc[a, :, part] += jnp.dot(held, wq[cols(q), part], preferred_element_type=F32)

    def qkv_kv(a, b, q):
        acc[a, :, pl.ds(512, 256)] += lax.dot_general(
            xs[b, :, cols(q)], wkv[:, cols(q)], transposed, preferred_element_type=F32
        )

    def qkv(a, b, q):
        qkv_q(a, b, q)
        qkv_kv(a, b, q)

    def table(ref, b):
        at = b * BLK
        far = at + (1 - zl) * 128
        parts = [ref[rows(at + zl * 128, 128), :]]
        for half in (1 - zl, zl):
            for core in range(2):
                parts.append(ref[rows(far + core * 64 + half * 32, 32), :])
        return jnp.concatenate(parts, axis=0)

    def kv_send(b):
        return remote(kvl.at[b, c], kvr.at[b, c], s_kvs.at[0, b], s_kvr.at[0, b], across)

    def kv_pass(b):
        return remote(kvr.at[b, c], kvr.at[b, c], s_kvs.at[1, b], s_kvr.at[1, b], sibling)

    def kv_wait(b):
        landed(kvr.at[b, 1 - c], s_kvr.at[1, b])

    def turned(value, b):
        lane = lax.broadcasted_iota(jnp.int32, (BLK, HD), 1)
        swapped = jnp.where(lane % 2 == 0, pltpu.roll(value, HD - 1, 1), pltpu.roll(value, 1, 1))
        return value * table(cos, b) + swapped * table(sin, b)

    def finish_kv(a, b):
        lane = lax.broadcasted_iota(jnp.int32, (BLK, HD), 1)
        first, second = acc[a, :, 512:640], acc[a, :, 640:768]
        key = turned(jnp.where(lane < 64, first, pltpu.roll(second, 64, 1)), b).astype(BF16)
        value = jnp.where(lane < 64, pltpu.roll(first, 64, 1), second).T.astype(BF16)
        for half in range(2):
            kvl[b, half, 0:128] = key[half * 128 : half * 128 + 128]
            kvl[b, half, 128:256] = value[:, half * 128 : half * 128 + 128]
        kv_send(b).start()

    def finish_q(a, b):
        scale = HD**-0.5 * math.log2(math.e)
        for h in range(HEADS):
            head = (turned(acc[a, :, h * HD : (h + 1) * HD], b) * scale).astype(BF16)
            qb[b, h * 192 : h * 192 + 192] = head[0:192]
            qb[b, 768 + h * 64 : 832 + h * 64] = head[192:256]

    def finish_qkv(a, b):
        finish_kv(a, b)
        finish_q(a, b)

    in_copies[2].wait()

    def first_loop(q, carry):
        @pl.when(q > 0)
        def _():
            for b, way in ((b_left, 0), (b_right, 1)):
                landed(part_ref(b, q, 0, c), s_xr.at[way, b, q])
                send_z(b, q)
                send_half(b, q, way)
                send_sib(b, q, 0)

        pass_z(b_own, q)
        wo_part(q).start()
        recv_sib(b_own, q)

        @pl.when(q == 0)
        def _():
            other = rows((1 - c) * HD, 64), rows((1 - c) * HD + 64, 64)
            landed(wkv.at[other[0]], s_w.at[3])
            landed(wkv.at[other[1]], s_w.at[4])

        qkv(2, b_own, q)
        return carry

    lax.fori_loop(0, NQ, first_loop, 0)
    for way in range(2):
        send_x(b_own, 0, way)
    for turn in range(2):
        for way in range(2):
            send_extra(b_own, 1 + (way + turn) % 2, way)
    in_copies[3].wait()
    in_copies[4].wait()
    finish_qkv(2, b_own)
    acc[2] = jnp.zeros((BLK, 768), F32)

    def both(fn):
        def one(a, carry):
            fn(a, (x + 1 + 2 * a) % 4)
            return carry

        lax.fori_loop(0, 2, one, 0)

    def far_rows(q):
        for way in range(2):
            landed(half_ref(b_far, q, way), s_xr.at[way, b_far, q])

    def second_loop(i, carry):
        q = i + 1
        for b in (b_left, b_right):
            pass_z(b, q)

        def near(a, b):
            recv_sib(b, q)
            qkv(a, b, q)

        both(near)
        far_rows(q)
        send_z(b_far, q)
        send_sib(b_far, q, 0)
        wo_part(4 + i).start()
        return carry

    lax.fori_loop(0, NQ - 1, second_loop, 0)

    def near_first(turn):
        for b, way in ((b_left, 0), (b_right, 1)):
            if turn == 0:
                landed(part_ref(b, 0, 0, c), s_xr.at[way, b, 0])
                send_half(b, 0, way)
                send_sib(b, 0, 0)
            else:
                kind = 1 + (way + turn - 1) % 2
                landed(part_ref(b, 0, kind, c), s_xe.at[kind - 1, b])
                if turn == 1:
                    send_extra(b, kind, way)
                send_sib(b, 0, kind)

    def third_loop(i, carry):
        for kind in range(3):
            pl.when(i == kind)(lambda kind=kind: near_first(kind))
        pass_z(b_far, i + 1)
        recv_sib(b_far, i + 1)
        qkv(2, b_far, i + 1)
        return carry

    lax.fori_loop(0, NQ - 1, third_loop, 0)
    kv_send(b_own).wait_recv()
    kv_pass(b_own).start()

    def near_last(a, b):
        recv_sib(b, 0)
        qkv(a, b, 0)
        finish_qkv(a, b)

    both(near_last)
    wo_part(7).start()
    far_rows(0)
    send_sib(b_far, 0, 0)
    for kind in (1, 2):
        landed(part_ref(b_far, 0, kind, c), s_xe.at[kind - 1, b_far])
        send_sib(b_far, 0, kind)
    recv_sib(b_far, 0)
    qkv_kv(2, b_far, 0)
    finish_kv(2, b_far)
    qkv_q(2, b_far, 0)
    finish_q(2, b_far)

    for b in (b_right, b_left):
        kv_send(b).wait_recv()
        kv_pass(b).start()
    for b in (b_own, b_right, b_left):
        kv_wait(b)

    def place(row):
        other = row >= 192
        inner = jnp.where(other, row - 192, row - 128)
        half = jnp.where(other, zl, 1 - zl)
        far = (1 - zl) * 128 + (inner // 32) * 64 + half * 32 + inner % 32
        return jnp.where(row < 128, zl * 128 + row, far)

    def attend_step(b, kb, state, masked):
        low = lax.broadcasted_iota(jnp.int32, (HD, HD), 1) < 64

        def joined(mine, theirs):
            key = jnp.concatenate([mine[kb, 0, 0:128], mine[kb, 1, 0:64], theirs[kb, 1, 64:128]], axis=0)
            half = jnp.where(low, mine[kb, 1, 128:256].astype(F32), theirs[kb, 1, 128:256].astype(F32))
            return key, jnp.concatenate([mine[kb, 0, 128:256], half.astype(BF16)], axis=1)

        inside, outside = joined(kvl, kvr), joined(kvr, kvl)
        after = []
        for group in range(0, NCH, NCH // 2):
            part = range(group, group + NCH // 2)
            sides = {j: inside if j * CHUNK < 768 else outside for j in part}
            scores = {
                j: lax.dot_general(
                    sides[j][0], qb[b, pl.ds(j * CHUNK, CHUNK)], transposed, preferred_element_type=F32
                )
                for j in part
            }
            if masked:
                column = lax.broadcasted_iota(jnp.int32, (1, CHUNK), 1)
                row = place(lax.broadcasted_iota(jnp.int32, (BLK, 1), 0))
                for j in part:
                    at = j * CHUNK
                    query = (column + at) % 192 if at < 768 else 192 + (column + at - 768) % 64
                    scores[j] = jnp.where(row <= place(query), scores[j], -1e30)
            tops = {
                j: jnp.maximum(state[j][0], jnp.max(scores[j], axis=0, keepdims=True)) for j in part
            }
            weights = {j: jnp.exp2(scores[j] - tops[j]) for j in part}
            for j in part:
                fade = jnp.exp2(state[j][0] - tops[j])
                whole = state[j][1] * fade + jnp.sum(weights[j], axis=0, keepdims=True)
                term = jnp.dot(sides[j][1], weights[j].astype(BF16), preferred_element_type=F32)
                after.append((tops[j], whole, state[j][2] * fade + term))
        return tuple(after)

    def attend(b, before_last=None):
        start = tuple(
            (jnp.full((1, CHUNK), -1e30, F32), jnp.zeros((1, CHUNK), F32), jnp.zeros((HD, CHUNK), F32))
            for _ in range(NCH)
        )
        state = lax.fori_loop(0, b, lambda kb, s: attend_step(b, kb, s, False), start)
        if before_last is not None:
            before_last()
        state = attend_step(b, b, state, True)
        out = [(value / whole).T.astype(BF16) for _, whole, value in state]
        inside, outside = jnp.concatenate(out[:6], axis=0), jnp.concatenate(out[6:], axis=0)
        for h in range(HEADS):
            at = pl.ds(h * HD, HD)
            for core in range(2):
                first, second = h * 192 + core * 64, h * 192 + 128 + core * 32
                third = h * 64 + core * 32
                ctx[b, core, 0:64, at] = inside[first : first + 64]
                ctx[b, core, 64:96, at] = inside[second : second + 32]
                ctx[b, core, 96:128, at] = outside[third : third + 32]
        ctx_send(b).start()

    def ctx_send(b):
        return remote(ctx.at[b, 1 - c], ctxr.at[b], s_ctx.at[0, b], s_ctx.at[1, b], sibling)

    def far_kv():
        kv_send(b_far).wait_recv()
        kv_pass(b_far).start()
        kv_wait(b_far)

    def third_cols(q):
        return pl.ds(pl.multiple_of((q - 1) * REST, REST), REST)

    def sum_cols(q):
        if isinstance(q, int) and q == 0:
            return pl.ds(0, FIRST)
        return pl.ds(pl.multiple_of(FIRST + (q - 1) * REST, 256), REST)

    def project(b, q):
        at = sum_cols(q)
        term = jnp.dot(ctx[b, c], wo[0, :, at], preferred_element_type=F32)
        term += jnp.dot(ctxr[b], wo[1, :, at], preferred_element_type=F32)
        xs[b, 0:128, at] = term.astype(BF16)

    def rs_z(b, q):
        for way in range(2):
            at = (64 + 32 * zl, 96 - 32 * zl)[way]
            place_in = pl.ds(32 - 32 * way, 32)
            dst = rz0.at[place_in] if isinstance(q, int) else rz.at[b, place_in, third_cols(q)]
            src = xs.at[b, rows(at, 32), sum_cols(q)]
            to = (above, below)[way]
            remote(src, dst, s_rsend.at[way, b], s_rz.at[way, b, q], to).start()

    def drain(b, kind):
        quarter, third = xs.at[b, 0:32], xs.at[b, 0:32, 0:THIRD]
        for way in range(2):
            sent(quarter if kind == "own" else third, s_send.at[2 + way, b])
        for part, ref in enumerate((xs.at[b, 0:64], quarter, quarter)):
            sent(ref, s_send.at[4 + part, b])
        if kind == "own":
            for way in range(2):
                sent(xs.at[b, 0:64], s_send.at[way, b])
                sent(xs.at[b, 0:64, 0:PIECE], s_send.at[7 + way, b])
        elif kind in (0, 1):
            sent(quarter, s_send.at[kind, b])
            sent(xs.at[b, 0:32, 0:PIECE], s_send.at[7 + kind, b])

    def sum_z(b, q):
        for way in range(2):
            landed(rz.at[b, pl.ds(32 - 32 * way, 32), third_cols(q)], s_rz.at[way, b, q])
        return xs[b, 0:64, sum_cols(q)].astype(F32) + rz[b, :, third_cols(q)].astype(F32)

    def relay(q, way):
        part = pl.ds(32 * way, 32)
        to = x_ways[way]
        src, dst = xs.at[b_far, part, sum_cols(q)], rr.at[way, :, sum_cols(q)]
        remote(src, dst, s_rsend.at[2 + way, b_far], s_rr.at[way, q], to).start()
        if isinstance(q, int):
            src = xs.at[b_far, pl.ds(64 + 32 * way, 32), sum_cols(0)]
            remote(src, rr0.at[way], s_rsend.at[4 + way, b_far], s_rr.at[way, NQ], to).start()

    def far_sum(q):
        xs[b_far, 0:64, sum_cols(q)] = sum_z(b_far, q).astype(BF16)
        relay(q, 0)
        relay(q, 1)

    def near_sum_first(way):
        b, to = (b_right, b_left)[way], x_ways[way]
        landed(rr.at[way, :, sum_cols(0)], s_rr.at[way, 0])
        landed(rr0.at[way], s_rr.at[way, NQ])
        for at, term in ((32 * way, rr[way, :, sum_cols(0)]), (64 + 32 * way, rr0[way])):
            total = xs[b, at : at + 32, sum_cols(0)].astype(F32) + term.astype(F32)
            xs[b, at : at + 32, sum_cols(0)] = total.astype(BF16)
        src = xs.at[b, 0:128, sum_cols(0)]
        remote(src, rx0.at[way], s_rsend.at[4 + way, b], s_rx.at[way, 0], to).start()

    def near_sum(q, way):
        b, to = (b_right, b_left)[way], x_ways[way]
        landed(rr.at[way, :, sum_cols(q)], s_rr.at[way, q])
        total = sum_z(b, q)
        term = rr[way, :, sum_cols(q)].astype(F32)
        first, second = total[0:32], total[32:64]
        if way == 0:
            first = first + term
        else:
            second = second + term
        xs[b, 0:32, sum_cols(q)] = first.astype(BF16)
        xs[b, 32:64, sum_cols(q)] = second.astype(BF16)
        dst = rx.at[way, :, third_cols(q)]
        remote(xs.at[b, 0:64, sum_cols(q)], dst, s_rsend.at[2 + way, b], s_rx.at[way, q], to).start()

    attend(b_far, far_kv)
    drain(b_far, "far")
    in_copies[5].wait()
    landed(wo.at[1], s_w.at[5])
    ctx_send(b_far).wait_recv()
    project(b_far, 0)
    relay(0, 0)
    relay(0, 1)

    def far_project(i, carry):
        project(b_far, i + 1)
        rs_z(b_far, i + 1)
        return carry

    lax.fori_loop(0, NQ - 1, far_project, 0)
    drain(b_right, 1)
    drain(b_left, 0)

    def near_project(a, b):
        attend(b)

        def sums(q, carry):
            far_sum(q)
            return carry

        lax.fori_loop(1 + a, 2 + 2 * a, sums, 0)
        ctx_send(b).wait_recv()

        def piece(q, carry):
            project(b, q)
            rs_z(b, q)
            return carry

        lax.fori_loop(1, 2, piece, 0)
        project(b, 0)
        for way in range(2):
            pl.when(a == way)(lambda way=way: near_sum_first(way))
        lax.fori_loop(2, NQ, piece, 0)

    both(near_project)
    attend(b_own)
    drain(b_own, "own")
    ctx_send(b_own).wait_recv()

    def own_project(q, carry):
        project(b_own, q)
        rs_z(b_own, q)
        near_sum(q, 0)
        near_sum(q, 1)
        return carry

    lax.fori_loop(1, NQ, own_project, 0)
    project(b_own, 0)

    landed(rx0.at[0], s_rx.at[0, 0])
    landed(rx0.at[1], s_rx.at[1, 0])
    whole = xs[b_own, 0:128, sum_cols(0)].astype(F32) + rx0[0].astype(F32) + rx0[1].astype(F32)
    xs[b_own, 0:128, sum_cols(0)] = whole.astype(BF16)
    rs_z(b_own, 0)

    def store(q, head_sum):
        at = sum_cols(q)
        tok[:, at] = (tok[:, at].astype(F32) + head_sum).astype(BF16)
        pltpu.make_async_copy(tok.at[:, at], out_hbm.at[:, at], s_out.at[q]).start()

    def last_sum(q):
        total = sum_z(b_own, q)
        for way in range(2):
            landed(rx.at[way, :, third_cols(q)], s_rx.at[way, q])
        total += rx[0, :, third_cols(q)].astype(F32) + rx[1, :, third_cols(q)].astype(F32)
        store(q, total)

    def last_two(i, carry):
        last_sum(i + 1)
        return carry

    lax.fori_loop(0, 2, last_two, 0)
    for way in range(2):
        landed(rz0.at[pl.ds(32 - 32 * way, 32)], s_rz.at[way, b_own, 0])
    store(0, xs[b_own, 0:64, sum_cols(0)].astype(F32) + rz0[...].astype(F32))
    lax.fori_loop(2, 3, last_two, 0)

    for q in range(NQ):
        pltpu.make_async_copy(tok.at[:, sum_cols(q)], out_hbm.at[:, sum_cols(q)], s_out.at[q]).wait()
    for copy in wkv_sends:
        copy.wait_send()
    sent(wo.at[1], s_w.at[2])
    for b in range(NX):
        kv_send(b).wait_send()
        kv_pass(b).wait_send()
        ctx_send(b).wait_send()
    for way in range(2):
        for b in (b_far, b_right, b_left):
            sent(xs.at[b, 0:32, 0 : 3 * REST], s_rsend.at[way, b])
        sent(xs.at[b_own, 0:32], s_rsend.at[way, b_own])
        sent(xs.at[b_far, 0:32], s_rsend.at[2 + way, b_far])
        sent(xs.at[b_far, 0:32, 0:FIRST], s_rsend.at[4 + way, b_far])
        b = (b_right, b_left)[way]
        sent(xs.at[b, 0:64, 0 : 3 * REST], s_rsend.at[2 + way, b])
        sent(xs.at[b, 0:128, 0:FIRST], s_rsend.at[4 + way, b])


def final_norm(stream_in, gain, stream_out, mlp_out):
    stream = stream_in[...]
    stream_out[...] = stream
    as_float = stream.astype(F32)
    inv = lax.rsqrt(jnp.mean(as_float * as_float, axis=-1, keepdims=True) + 1e-05)
    mlp_out[...] = (as_float * inv * gain[...].astype(F32)).astype(BF16)


def sublayer(tokens, gain_attn, w_query, w_key, w_value, w_out, gain_mlp):
    cos, sin = rotary_tables()
    gain_attn, gain_mlp = gain_attn.reshape(1, D), gain_mlp.reshape(1, D)
    any_spec = pl.BlockSpec(memory_space=pl.ANY)
    vmem_spec = pl.BlockSpec(memory_space=pltpu.VMEM)
    dma = pltpu.SemaphoreType.DMA
    shape = jax.ShapeDtypeStruct((64, D), BF16)
    stream = pl.pallas_call(
        kernel,
        out_shape=shape,
        in_specs=[any_spec, vmem_spec] + [any_spec] * 6,
        out_specs=any_spec,
        scratch_shapes=[
            pltpu.VMEM((NX, BLK, D), BF16),
            pltpu.VMEM((D, 512), BF16),
            pltpu.VMEM((256, D), BF16),
            pltpu.VMEM((2, 512, D), BF16),
            pltpu.VMEM((NX, HEADS * BLK, HD), BF16),
            pltpu.VMEM((NX, 2, 256, HD), BF16),
            pltpu.VMEM((NX, 2, 256, HD), BF16),
            pltpu.VMEM((NX, 2, 128, 512), BF16),
            pltpu.VMEM((NX, 128, 512), BF16),
            pltpu.VMEM((3, BLK, 768), F32),
            pltpu.VMEM((NX * BLK, HD), F32),
            pltpu.VMEM((NX * BLK, HD), F32),
            pltpu.VMEM((NX, 64, 3 * REST), BF16),
            pltpu.VMEM((64, FIRST), BF16),
            pltpu.VMEM((2, 32, D), BF16),
            pltpu.VMEM((2, 32, FIRST), BF16),
            pltpu.VMEM((2, 64, 3 * REST), BF16),
            pltpu.VMEM((2, 128, FIRST), BF16),
            pltpu.VMEM((64, D), BF16),
            dma((7,)),
            dma((9, NX)),
            dma((2, NX, NQ)),
            dma((2, NX)),
            dma((2, NX, NQ)),
            dma((3, NX, NQ)),
            dma((6,)),
            dma((2, NX)),
            dma((2, NX)),
            dma((2, NX)),
            dma((6, NX)),
            dma((2, NX, NQ)),
            dma((2, NQ + 1)),
            dma((2, NQ)),
            dma((NQ,)),
        ],
        compiler_params=pltpu.CompilerParams(
            collective_id=0, has_side_effects=True, vmem_limit_bytes=63 * 2**20
        ),
        cost_estimate=pl.CostEstimate(
            flops=24_000_000_000, bytes_accessed=24_000_000, transcendentals=4_000_000
        ),
    )(
        tokens, gain_attn, w_query, w_key.T, w_value.T, w_out, jnp.asarray(cos), jnp.asarray(sin),
    )
    block = pl.BlockSpec((16, D), lambda i: (i, 0))
    return pl.pallas_call(
        final_norm,
        grid=(4,),
        out_shape=(shape, shape),
        in_specs=[block, pl.BlockSpec((1, D), lambda i: (0, 0))],
        out_specs=(block, block),
        compiler_params=pltpu.CompilerParams(vmem_limit_bytes=60 * 2**20),
        cost_estimate=pl.CostEstimate(flops=3_000_000, bytes_accessed=3_000_000, transcendentals=64),
    )(stream, gain_mlp)


def solution(mesh):
    placed = (
        P(("dp", "tp"), None),
        P(),
        P(None, "tp"),
        P(None, "tp"),
        P(None, "tp"),
        P("tp", None),
        P(),
    )
    return jax.shard_map(
        sublayer,
        mesh=mesh,
        in_specs=placed,
        out_specs=(P(("dp", "tp"), None), P(("dp", "tp"), None)),
        check_vma=False,
    )
```

```python
import math

import jax
import jax.numpy as jnp
import numpy as np
from jax import lax
from jax.experimental import pallas as pl
from jax.experimental.pallas import tpu as pltpu
from jax.sharding import PartitionSpec as P

MESH = pl.DeviceIdType.MESH
BF16 = jnp.bfloat16
F32 = jnp.float32
D = 8192
HD = 128
NX = 4
BLK = 256
PIECE = 2048
NQ = D // PIECE
HEADS = 4
THIRD = D - PIECE
FIRST = 1280
REST = (D - FIRST) // 3
WO_PARTS = 8
REST_OF_ROW = (1, 2, 3)
NCH = 8
CHUNK = HEADS * BLK // NCH


def rotary_tables():
    inverse = np.exp(np.arange(HD // 2) * (-2.0 * math.log(500000.0) / HD))
    angles = np.arange(NX * BLK)[:, None] * inverse[None, :]
    cos = np.repeat(np.cos(angles), 2, axis=1).astype(np.float32)
    sin = np.repeat(np.sin(angles), 2, axis=1)
    sin[:, 0::2] *= -1.0
    return cos, sin.astype(np.float32)


def kernel(
    tok_hbm, gains, wq_hbm, wk_hbm, wv_hbm, wo_hbm, cos_hbm, sin_hbm, out_hbm,
    xs, wq, wkv, wo, qb, kvl, kvr, ctx, ctxr, acc, cos, sin, rz, rz0, rr, rr0, rx, rx0, tok,
    s_in, s_send, s_xr, s_xf, s_xe, s_zr, s_sib, s_w, s_kvs, s_kvr, s_ctx, s_rsend, s_rz, s_rr, s_rx, s_out,
):
    tp, dp = lax.axis_index("tp"), lax.axis_index("dp")
    x, zl, c = tp // 4, (tp // 2) % 2, tp % 2
    y, zz = dp // 2, (dp % 2) * 2 + zl

    def device(x_to, z_to, c_to):
        return (x_to * 4 + (z_to % 2) * 2 + c_to, y * 2 + z_to // 2)

    right, left = device((x + 1) % 4, zz, c), device((x + 3) % 4, zz, c)
    above, below = device(x, (zz + 1) % 4, c), device(x, (zz + 3) % 4, c)
    across, sibling = device(x, (zz + 2) % 4, c), device(x, zz, 1 - c)
    b_own, b_right, b_far, b_left = x, (x + 1) % 4, (x + 2) % 4, (x + 3) % 4

    def remote(src, dst, send_sem, recv_sem, to):
        return pltpu.make_async_remote_copy(
            src_ref=src, dst_ref=dst, send_sem=send_sem, recv_sem=recv_sem,
            device_id=to, device_id_type=MESH,
        )

    def sent(ref, sem):
        remote(ref, ref, sem, s_w.at[0], sibling).wait_send()

    def landed(ref, sem):
        remote(ref, ref, s_w.at[0], sem, sibling).wait_recv()

    def cols(q):
        if q is REST_OF_ROW:
            return pl.ds(PIECE, THIRD)
        return pl.ds(pl.multiple_of(q * PIECE, PIECE), PIECE)

    def sem_at(q):
        return 1 if q is REST_OF_ROW else q

    def rows(start, size):
        return pl.ds(pl.multiple_of(start, 32), size)

    tok_copy = pltpu.make_async_copy(tok_hbm, tok, s_in.at[0])
    tok_copy.start()
    barrier = pltpu.get_barrier_semaphore()
    for neighbour in (right, left, above, below, across, sibling):
        pl.semaphore_signal(barrier, inc=1, device_id=neighbour, device_id_type=MESH)

    wk_rows, wv_rows = rows(c * HD, 64), rows(c * HD + 64, 64)
    in_copies = [
        pltpu.make_async_copy(wk_hbm, wkv.at[wk_rows], s_in.at[1]),
        pltpu.make_async_copy(wv_hbm, wkv.at[wv_rows], s_in.at[2]),
        pltpu.make_async_copy(wq_hbm, wq, s_in.at[3]),
        pltpu.make_async_copy(cos_hbm, cos, s_in.at[4]),
        pltpu.make_async_copy(sin_hbm, sin, s_in.at[5]),
        pltpu.make_async_copy(wo_hbm, wo.at[0], s_in.at[6]),
    ]
    for copy in in_copies:
        copy.start()

    tok_copy.wait()

    def norm_rows(i, carry):
        part = pl.ds(pl.multiple_of(i * 16, 16), 16)
        as_float = tok[part, :].astype(F32)
        inv = lax.rsqrt(jnp.mean(as_float * as_float, axis=-1, keepdims=True) + 1e-05)
        normed = as_float * inv * gains[...].astype(F32)
        xs[x, pl.ds(pl.multiple_of(c * 64 + i * 16, 16), 16), :] = normed.astype(BF16)
        return carry

    lax.fori_loop(0, 4, norm_rows, 0)
    pl.semaphore_wait(barrier, 6)

    from_below = 192 - 64 * zl
    from_above = 128 + 64 * zl
    x_ways = (right, left)

    def part_ref(b, q, kind, core):
        if kind == 0:
            return xs.at[b, rows(core * 64, 64), cols(q)]
        at = (from_below, from_above)[kind - 1]
        return xs.at[b, rows(at + core * 32, 32), cols(q)]

    def half_ref(b, q, way):
        return xs.at[b, rows(c * 64 + 32 * way, 32), cols(q)]

    def send_x(b, q, way):
        ref = part_ref(b, q, 0, c)
        remote(ref, ref, s_send.at[way, b], s_xr.at[way, b, q], x_ways[way]).start()

    def send_half(b, q, way):
        ref = half_ref(b, q, way)
        remote(ref, ref, s_send.at[way, b], s_xf.at[q], x_ways[way]).start()

    def send_extra(b, kind, way):
        ref = part_ref(b, 0, kind, c)
        remote(ref, ref, s_send.at[7 + way, b], s_xe.at[kind - 1, b], x_ways[way]).start()

    def send_z(b, q):
        for way in range(2):
            at = (from_above, from_below)[way]
            dst = xs.at[b, rows(at + c * 32, 32), cols(q)]
            to = (above, below)[way]
            remote(half_ref(b, q, way), dst, s_send.at[2 + way, b], s_zr.at[b, sem_at(q)], to).start()

    def send_sib(b, q, kind):
        ref = part_ref(b, q, kind, c)
        remote(ref, ref, s_send.at[4 + kind, b], s_sib.at[b, sem_at(q)], sibling).start()

    def recv_sib(b, q):
        landed(xs.at[b, 0:128, cols(q)], s_sib.at[b, sem_at(q)])

    def pass_z(b, q):
        landed(xs.at[b, 0:64, cols(q)], s_zr.at[b, sem_at(q)])
        send_sib(b, q, 1)
        send_sib(b, q, 2)

    send_z(b_own, 0)
    for q in range(1, NQ):
        send_x(b_own, q, 0)
        send_x(b_own, q, 1)
        if q == 1:
            send_z(b_own, REST_OF_ROW)
            send_sib(b_own, 0, 0)
            send_sib(b_own, REST_OF_ROW, 0)
    in_copies[0].wait()
    in_copies[1].wait()
    wkv_sends = [
        remote(wkv.at[wk_rows], wkv.at[wk_rows], s_w.at[0], s_w.at[3], sibling),
        remote(wkv.at[wv_rows], wkv.at[wv_rows], s_w.at[1], s_w.at[4], sibling),
    ]
    for copy in wkv_sends:
        copy.start()

    def wo_part(k):
        part = rows(k * (512 // WO_PARTS), 512 // WO_PARTS)
        return remote(wo_hbm.at[part], wo.at[1, part], s_w.at[2], s_w.at[5], sibling)

    acc[...] = jnp.zeros_like(acc)
    transposed = (((1,), (1,)), ((), ()))

    def qkv_q(a, b, q):
        held = xs[b, :, cols(q)]
        for n in range(2):
            part = pl.ds(n * 256, 256)
            acc[a, :, part] += jnp.dot(held, wq[cols(q), part], preferred_element_type=F32)

    def qkv_kv(a, b, q):
        acc[a, :, pl.ds(512, 256)] += lax.dot_general(
            xs[b, :, cols(q)], wkv[:, cols(q)], transposed, preferred_element_type=F32
        )

    def qkv(a, b, q):
        qkv_q(a, b, q)
        qkv_kv(a, b, q)

    def table(ref, b):
        at = b * BLK
        far = at + (1 - zl) * 128
        parts = [ref[rows(at + zl * 128, 128), :]]
        for half in (1 - zl, zl):
            for core in range(2):
                parts.append(ref[rows(far + core * 64 + half * 32, 32), :])
        return jnp.concatenate(parts, axis=0)

    def kv_send(b):
        return remote(kvl.at[b, c], kvr.at[b, c], s_kvs.at[0, b], s_kvr.at[0, b], across)

    def kv_pass(b):
        return remote(kvr.at[b, c], kvr.at[b, c], s_kvs.at[1, b], s_kvr.at[1, b], sibling)

    def kv_wait(b):
        landed(kvr.at[b, 1 - c], s_kvr.at[1, b])

    def turned(value, b):
        lane = lax.broadcasted_iota(jnp.int32, (BLK, HD), 1)
        swapped = jnp.where(lane % 2 == 0, pltpu.roll(value, HD - 1, 1), pltpu.roll(value, 1, 1))
        return value * table(cos, b) + swapped * table(sin, b)

    def finish_kv(a, b):
        lane = lax.broadcasted_iota(jnp.int32, (BLK, HD), 1)
        first, second = acc[a, :, 512:640], acc[a, :, 640:768]
        key = turned(jnp.where(lane < 64, first, pltpu.roll(second, 64, 1)), b).astype(BF16)
        value = jnp.where(lane < 64, pltpu.roll(first, 64, 1), second).T.astype(BF16)
        for half in range(2):
            kvl[b, half, 0:128] = key[half * 128 : half * 128 + 128]
            kvl[b, half, 128:256] = value[:, half * 128 : half * 128 + 128]
        kv_send(b).start()

    def finish_q(a, b):
        scale = HD**-0.5 * math.log2(math.e)
        for h in range(HEADS):
            head = (turned(acc[a, :, h * HD : (h + 1) * HD], b) * scale).astype(BF16)
            qb[b, h * 192 : h * 192 + 192] = head[0:192]
            qb[b, 768 + h * 64 : 832 + h * 64] = head[192:256]

    def finish_qkv(a, b):
        finish_kv(a, b)
        finish_q(a, b)

    in_copies[2].wait()

    def near_piece(q, carry):
        for b, way in ((b_left, 0), (b_right, 1)):
            landed(part_ref(b, q, 0, c), s_xr.at[way, b, q])
            send_z(b, q)
            send_half(b, q, way)
            send_sib(b, q, 0)
        wo_part(q - 1).start()
        return carry

    pass_z(b_own, 0)
    landed(wkv.at[rows((1 - c) * HD, 64)], s_w.at[3])
    landed(wkv.at[rows((1 - c) * HD + 64, 64)], s_w.at[4])
    recv_sib(b_own, 0)
    qkv(2, b_own, 0)
    lax.fori_loop(1, 3, near_piece, 0)
    pass_z(b_own, REST_OF_ROW)
    recv_sib(b_own, REST_OF_ROW)
    qkv(2, b_own, REST_OF_ROW)
    lax.fori_loop(3, 4, near_piece, 0)
    for way in range(2):
        send_x(b_own, 0, way)
    for turn in range(2):
        for way in range(2):
            send_extra(b_own, 1 + (way + turn) % 2, way)
    in_copies[3].wait()
    in_copies[4].wait()
    finish_qkv(2, b_own)
    acc[2] = jnp.zeros((BLK, 768), F32)

    def both(fn):
        def one(a, carry):
            fn(a, (x + 1 + 2 * a) % 4)
            return carry

        lax.fori_loop(0, 2, one, 0)

    def far_rows(q):
        landed(part_ref(b_far, q, 0, c), s_xf.at[q])
        send_sib(b_far, q, 0)

    def far_spread(q):
        far_rows(q)
        send_z(b_far, q)

    def second_loop(i, carry):
        q = i + 1

        @pl.when(i == 1)
        def _():
            far_spread(1)
            far_spread(2)

        @pl.when(i == 2)
        def _():
            far_spread(3)

        for b in (b_left, b_right):
            pass_z(b, q)

        def near(a, b):
            recv_sib(b, q)
            qkv_kv(a, b, q)

        both(near)
        wo_part(3 + i).start()
        return carry

    lax.fori_loop(0, NQ - 1, second_loop, 0)

    def near_first(turn):
        for b, way in ((b_left, 0), (b_right, 1)):
            if turn == 0:
                landed(part_ref(b, 0, 0, c), s_xr.at[way, b, 0])
                send_half(b, 0, way)
                send_sib(b, 0, 0)
            else:
                kind = 1 + (way + turn - 1) % 2
                landed(part_ref(b, 0, kind, c), s_xe.at[kind - 1, b])
                if turn == 1:
                    send_extra(b, kind, way)
                send_sib(b, 0, kind)

    def third_loop(i, carry):
        for kind in range(3):
            pl.when(i == kind)(lambda kind=kind: near_first(kind))
        pass_z(b_far, i + 1)
        recv_sib(b_far, i + 1)
        qkv(2, b_far, i + 1)
        return carry

    lax.fori_loop(0, NQ - 1, third_loop, 0)
    kv_send(b_own).wait_recv()
    kv_pass(b_own).start()

    def near_last(a, b):
        recv_sib(b, 0)
        qkv_kv(a, b, 0)
        finish_kv(a, b)

    both(near_last)
    wo_part(6).start()
    wo_part(7).start()
    far_rows(0)
    for kind in (1, 2):
        landed(part_ref(b_far, 0, kind, c), s_xe.at[kind - 1, b_far])
        send_sib(b_far, 0, kind)
    recv_sib(b_far, 0)
    qkv_kv(2, b_far, 0)
    finish_kv(2, b_far)
    qkv_q(2, b_far, 0)
    finish_q(2, b_far)

    for b in (b_right, b_left):
        kv_send(b).wait_recv()
        kv_pass(b).start()
    for b in (b_own, b_right, b_left):
        kv_wait(b)

    def place(row):
        other = row >= 192
        inner = jnp.where(other, row - 192, row - 128)
        half = jnp.where(other, zl, 1 - zl)
        far = (1 - zl) * 128 + (inner // 32) * 64 + half * 32 + inner % 32
        return jnp.where(row < 128, zl * 128 + row, far)

    def attend_step(b, kb, state, masked):
        low = lax.broadcasted_iota(jnp.int32, (HD, HD), 1) < 64

        def joined(mine, theirs):
            key = jnp.concatenate([mine[kb, 0, 0:128], mine[kb, 1, 0:64], theirs[kb, 1, 64:128]], axis=0)
            half = jnp.where(low, mine[kb, 1, 128:256].astype(F32), theirs[kb, 1, 128:256].astype(F32))
            return key, jnp.concatenate([mine[kb, 0, 128:256], half.astype(BF16)], axis=1)

        inside, outside = joined(kvl, kvr), joined(kvr, kvl)
        after = []
        for group in range(0, NCH, NCH // 2):
            part = range(group, group + NCH // 2)
            sides = {j: inside if j * CHUNK < 768 else outside for j in part}
            scores = {
                j: lax.dot_general(
                    sides[j][0], qb[b, pl.ds(j * CHUNK, CHUNK)], transposed, preferred_element_type=F32
                )
                for j in part
            }
            if masked:
                column = lax.broadcasted_iota(jnp.int32, (1, CHUNK), 1)
                row = place(lax.broadcasted_iota(jnp.int32, (BLK, 1), 0))
                for j in part:
                    at = j * CHUNK
                    query = (column + at) % 192 if at < 768 else 192 + (column + at - 768) % 64
                    scores[j] = jnp.where(row <= place(query), scores[j], -1e30)
            tops = {
                j: jnp.maximum(state[j][0], jnp.max(scores[j], axis=0, keepdims=True)) for j in part
            }
            weights = {j: jnp.exp2(scores[j] - tops[j]) for j in part}
            for j in part:
                fade = jnp.exp2(state[j][0] - tops[j])
                whole = state[j][1] * fade + jnp.sum(weights[j], axis=0, keepdims=True)
                term = jnp.dot(sides[j][1], weights[j].astype(BF16), preferred_element_type=F32)
                after.append((tops[j], whole, state[j][2] * fade + term))
        return tuple(after)

    def attend(b, before_last=None):
        start = tuple(
            (jnp.full((1, CHUNK), -1e30, F32), jnp.zeros((1, CHUNK), F32), jnp.zeros((HD, CHUNK), F32))
            for _ in range(NCH)
        )
        state = lax.fori_loop(0, b, lambda kb, s: attend_step(b, kb, s, False), start)
        if before_last is not None:
            before_last()
        state = attend_step(b, b, state, True)
        out = [(value / whole).T.astype(BF16) for _, whole, value in state]
        inside, outside = jnp.concatenate(out[:6], axis=0), jnp.concatenate(out[6:], axis=0)
        for h in range(HEADS):
            at = pl.ds(h * HD, HD)
            for core in range(2):
                first, second = h * 192 + core * 64, h * 192 + 128 + core * 32
                third = h * 64 + core * 32
                ctx[b, core, 0:64, at] = inside[first : first + 64]
                ctx[b, core, 64:96, at] = inside[second : second + 32]
                ctx[b, core, 96:128, at] = outside[third : third + 32]
        ctx_send(b).start()

    def ctx_send(b):
        return remote(ctx.at[b, 1 - c], ctxr.at[b], s_ctx.at[0, b], s_ctx.at[1, b], sibling)

    def far_kv():
        kv_send(b_far).wait_recv()
        kv_pass(b_far).start()
        kv_wait(b_far)

    def third_cols(q):
        return pl.ds(pl.multiple_of((q - 1) * REST, REST), REST)

    def sum_cols(q):
        if isinstance(q, int) and q == 0:
            return pl.ds(0, FIRST)
        return pl.ds(pl.multiple_of(FIRST + (q - 1) * REST, 256), REST)

    def project(b, q):
        at = sum_cols(q)
        term = jnp.dot(ctx[b, c], wo[0, :, at], preferred_element_type=F32)
        term += jnp.dot(ctxr[b], wo[1, :, at], preferred_element_type=F32)
        xs[b, 0:128, at] = term.astype(BF16)

    def rs_z(b, q):
        for way in range(2):
            at = (64 + 32 * zl, 96 - 32 * zl)[way]
            place_in = pl.ds(32 - 32 * way, 32)
            dst = rz0.at[place_in] if isinstance(q, int) else rz.at[b, place_in, third_cols(q)]
            src = xs.at[b, rows(at, 32), sum_cols(q)]
            to = (above, below)[way]
            remote(src, dst, s_rsend.at[way, b], s_rz.at[way, b, q], to).start()

    def drain(b, kind):
        quarter, third = xs.at[b, 0:32], xs.at[b, 0:32, 0:THIRD]
        for way in range(2):
            sent(quarter if kind == "own" else third, s_send.at[2 + way, b])
        for part, ref in enumerate((xs.at[b, 0:64], quarter, quarter)):
            sent(ref, s_send.at[4 + part, b])
        if kind == "own":
            for way in range(2):
                sent(xs.at[b, 0:64], s_send.at[way, b])
                sent(xs.at[b, 0:64, 0:PIECE], s_send.at[7 + way, b])
        elif kind in (0, 1):
            sent(quarter, s_send.at[kind, b])
            sent(xs.at[b, 0:32, 0:PIECE], s_send.at[7 + kind, b])

    def sum_z(b, q):
        for way in range(2):
            landed(rz.at[b, pl.ds(32 - 32 * way, 32), third_cols(q)], s_rz.at[way, b, q])
        return xs[b, 0:64, sum_cols(q)].astype(F32) + rz[b, :, third_cols(q)].astype(F32)

    def relay(q, way):
        part = pl.ds(32 * way, 32)
        to = x_ways[way]
        src, dst = xs.at[b_far, part, sum_cols(q)], rr.at[way, :, sum_cols(q)]
        remote(src, dst, s_rsend.at[2 + way, b_far], s_rr.at[way, q], to).start()
        if isinstance(q, int):
            src = xs.at[b_far, pl.ds(64 + 32 * way, 32), sum_cols(0)]
            remote(src, rr0.at[way], s_rsend.at[4 + way, b_far], s_rr.at[way, NQ], to).start()

    def far_sum(q):
        xs[b_far, 0:64, sum_cols(q)] = sum_z(b_far, q).astype(BF16)
        relay(q, 0)
        relay(q, 1)

    def near_sum_first(way):
        b, to = (b_right, b_left)[way], x_ways[way]
        landed(rr.at[way, :, sum_cols(0)], s_rr.at[way, 0])
        landed(rr0.at[way], s_rr.at[way, NQ])
        for at, term in ((32 * way, rr[way, :, sum_cols(0)]), (64 + 32 * way, rr0[way])):
            total = xs[b, at : at + 32, sum_cols(0)].astype(F32) + term.astype(F32)
            xs[b, at : at + 32, sum_cols(0)] = total.astype(BF16)
        src = xs.at[b, 0:128, sum_cols(0)]
        remote(src, rx0.at[way], s_rsend.at[4 + way, b], s_rx.at[way, 0], to).start()

    def near_sum(q, way):
        b, to = (b_right, b_left)[way], x_ways[way]
        landed(rr.at[way, :, sum_cols(q)], s_rr.at[way, q])
        total = sum_z(b, q)
        term = rr[way, :, sum_cols(q)].astype(F32)
        first, second = total[0:32], total[32:64]
        if way == 0:
            first = first + term
        else:
            second = second + term
        xs[b, 0:32, sum_cols(q)] = first.astype(BF16)
        xs[b, 32:64, sum_cols(q)] = second.astype(BF16)
        dst = rx.at[way, :, third_cols(q)]
        remote(xs.at[b, 0:64, sum_cols(q)], dst, s_rsend.at[2 + way, b], s_rx.at[way, q], to).start()

    attend(b_far, far_kv)
    drain(b_far, "far")
    in_copies[5].wait()
    landed(wo.at[1], s_w.at[5])
    ctx_send(b_far).wait_recv()
    project(b_far, 0)
    relay(0, 0)
    relay(0, 1)

    def far_project(i, carry):
        project(b_far, i + 1)
        rs_z(b_far, i + 1)
        return carry

    lax.fori_loop(0, NQ - 1, far_project, 0)
    drain(b_right, 1)
    drain(b_left, 0)

    def near_project(a, b):
        def sums(q, carry):
            far_sum(q)
            return carry

        def late_q(q, carry):
            qkv_q(a, b, q)
            return carry

        lax.fori_loop(0, NQ, late_q, 0)
        finish_q(a, b)
        lax.fori_loop(3, 3 + a, sums, 0)
        attend(b)
        lax.fori_loop(1, 2 - a, sums, 0)
        ctx_send(b).wait_recv()

        def piece(q, carry):
            project(b, q)
            rs_z(b, q)
            return carry

        lax.fori_loop(1, 2, piece, 0)
        project(b, 0)
        for way in range(2):
            pl.when(a == way)(lambda way=way: near_sum_first(way))
        lax.fori_loop(2, 3 - a, sums, 0)
        lax.fori_loop(2, NQ, piece, 0)

    both(near_project)
    attend(b_own)
    drain(b_own, "own")
    ctx_send(b_own).wait_recv()

    def own_project(q, carry):
        project(b_own, q)
        rs_z(b_own, q)
        near_sum(q, 0)
        near_sum(q, 1)
        return carry

    lax.fori_loop(1, NQ, own_project, 0)
    project(b_own, 0)

    landed(rx0.at[0], s_rx.at[0, 0])
    landed(rx0.at[1], s_rx.at[1, 0])
    whole = xs[b_own, 0:128, sum_cols(0)].astype(F32) + rx0[0].astype(F32) + rx0[1].astype(F32)
    xs[b_own, 0:128, sum_cols(0)] = whole.astype(BF16)
    rs_z(b_own, 0)

    def store(q, head_sum):
        at = sum_cols(q)
        tok[:, at] = (tok[:, at].astype(F32) + head_sum).astype(BF16)
        pltpu.make_async_copy(tok.at[:, at], out_hbm.at[:, at], s_out.at[q]).start()

    def last_sum(q):
        total = sum_z(b_own, q)
        for way in range(2):
            landed(rx.at[way, :, third_cols(q)], s_rx.at[way, q])
        total += rx[0, :, third_cols(q)].astype(F32) + rx[1, :, third_cols(q)].astype(F32)
        store(q, total)

    def last_two(i, carry):
        last_sum(i + 1)
        return carry

    lax.fori_loop(0, 2, last_two, 0)
    for way in range(2):
        landed(rz0.at[pl.ds(32 - 32 * way, 32)], s_rz.at[way, b_own, 0])
    store(0, xs[b_own, 0:64, sum_cols(0)].astype(F32) + rz0[...].astype(F32))
    lax.fori_loop(2, 3, last_two, 0)

    for q in range(NQ):
        pltpu.make_async_copy(tok.at[:, sum_cols(q)], out_hbm.at[:, sum_cols(q)], s_out.at[q]).wait()
    for copy in wkv_sends:
        copy.wait_send()
    sent(wo.at[1], s_w.at[2])
    for b in range(NX):
        kv_send(b).wait_send()
        kv_pass(b).wait_send()
        ctx_send(b).wait_send()
    for way in range(2):
        for b in (b_far, b_right, b_left):
            sent(xs.at[b, 0:32, 0 : 3 * REST], s_rsend.at[way, b])
        sent(xs.at[b_own, 0:32], s_rsend.at[way, b_own])
        sent(xs.at[b_far, 0:32], s_rsend.at[2 + way, b_far])
        sent(xs.at[b_far, 0:32, 0:FIRST], s_rsend.at[4 + way, b_far])
        b = (b_right, b_left)[way]
        sent(xs.at[b, 0:64, 0 : 3 * REST], s_rsend.at[2 + way, b])
        sent(xs.at[b, 0:128, 0:FIRST], s_rsend.at[4 + way, b])


def final_norm(stream_in, gain, stream_out, mlp_out):
    stream = stream_in[...]
    stream_out[...] = stream
    as_float = stream.astype(F32)
    inv = lax.rsqrt(jnp.mean(as_float * as_float, axis=-1, keepdims=True) + 1e-05)
    mlp_out[...] = (as_float * inv * gain[...].astype(F32)).astype(BF16)


def sublayer(tokens, gain_attn, w_query, w_key, w_value, w_out, gain_mlp):
    cos, sin = rotary_tables()
    gain_attn, gain_mlp = gain_attn.reshape(1, D), gain_mlp.reshape(1, D)
    any_spec = pl.BlockSpec(memory_space=pl.ANY)
    vmem_spec = pl.BlockSpec(memory_space=pltpu.VMEM)
    dma = pltpu.SemaphoreType.DMA
    shape = jax.ShapeDtypeStruct((64, D), BF16)
    stream = pl.pallas_call(
        kernel,
        out_shape=shape,
        in_specs=[any_spec, vmem_spec] + [any_spec] * 6,
        out_specs=any_spec,
        scratch_shapes=[
            pltpu.VMEM((NX, BLK, D), BF16),
            pltpu.VMEM((D, 512), BF16),
            pltpu.VMEM((256, D), BF16),
            pltpu.VMEM((2, 512, D), BF16),
            pltpu.VMEM((NX, HEADS * BLK, HD), BF16),
            pltpu.VMEM((NX, 2, 256, HD), BF16),
            pltpu.VMEM((NX, 2, 256, HD), BF16),
            pltpu.VMEM((NX, 2, 128, 512), BF16),
            pltpu.VMEM((NX, 128, 512), BF16),
            pltpu.VMEM((3, BLK, 768), F32),
            pltpu.VMEM((NX * BLK, HD), F32),
            pltpu.VMEM((NX * BLK, HD), F32),
            pltpu.VMEM((NX, 64, 3 * REST), BF16),
            pltpu.VMEM((64, FIRST), BF16),
            pltpu.VMEM((2, 32, D), BF16),
            pltpu.VMEM((2, 32, FIRST), BF16),
            pltpu.VMEM((2, 64, 3 * REST), BF16),
            pltpu.VMEM((2, 128, FIRST), BF16),
            pltpu.VMEM((64, D), BF16),
            dma((7,)),
            dma((9, NX)),
            dma((2, NX, NQ)),
            dma((NQ,)),
            dma((2, NX)),
            dma((NX, NQ)),
            dma((NX, NQ)),
            dma((6,)),
            dma((2, NX)),
            dma((2, NX)),
            dma((2, NX)),
            dma((6, NX)),
            dma((2, NX, NQ)),
            dma((2, NQ + 1)),
            dma((2, NQ)),
            dma((NQ,)),
        ],
        compiler_params=pltpu.CompilerParams(
            collective_id=0, has_side_effects=True, vmem_limit_bytes=63 * 2**20
        ),
        cost_estimate=pl.CostEstimate(
            flops=24_000_000_000, bytes_accessed=24_000_000, transcendentals=4_000_000
        ),
    )(
        tokens, gain_attn, w_query, w_key.T, w_value.T, w_out, jnp.asarray(cos), jnp.asarray(sin),
    )
    block = pl.BlockSpec((16, D), lambda i: (i, 0))
    return pl.pallas_call(
        final_norm,
        grid=(4,),
        out_shape=(shape, shape),
        in_specs=[block, pl.BlockSpec((1, D), lambda i: (0, 0))],
        out_specs=(block, block),
        compiler_params=pltpu.CompilerParams(vmem_limit_bytes=8 * 2**20),
        cost_estimate=pl.CostEstimate(flops=3_000_000, bytes_accessed=3_000_000, transcendentals=64),
    )(stream, gain_mlp)


def solution(mesh):
    placed = (
        P(("dp", "tp"), None),
        P(),
        P(None, "tp"),
        P(None, "tp"),
        P(None, "tp"),
        P("tp", None),
        P(),
    )
    return jax.shard_map(
        sublayer,
        mesh=mesh,
        in_specs=placed,
        out_specs=(P(("dp", "tp"), None), P(("dp", "tp"), None)),
        check_vma=False,
    )
```

```python
import math

import jax
import jax.numpy as jnp
import numpy as np
from jax import lax
from jax.experimental import pallas as pl
from jax.experimental.pallas import tpu as pltpu
from jax.sharding import PartitionSpec as P

MESH = pl.DeviceIdType.MESH
BF16 = jnp.bfloat16
F32 = jnp.float32
D = 8192
HD = 128
NX = 4
BLK = 256
PIECE = 2048
NQ = D // PIECE
HEADS = 4
THIRD = D - PIECE
FIRST = 1280
REST = (D - FIRST) // 3
WO_PARTS = 8
REST_OF_ROW = (1, 2, 3)
NCH = 8
CHUNK = HEADS * BLK // NCH


def scaled(value, gain):
    factor = gain[...].astype(F32)
    parts = [value[:, k * HD : (k + 1) * HD] * factor[k : k + 1] for k in range(D // HD)]
    return jnp.concatenate(parts, axis=1)


def rotary_tables():
    inverse = np.exp(np.arange(HD // 2) * (-2.0 * math.log(500000.0) / HD))
    angles = np.arange(NX * BLK)[:, None] * inverse[None, :]
    cos = np.repeat(np.cos(angles), 2, axis=1).astype(np.float32)
    sin = np.repeat(np.sin(angles), 2, axis=1)
    sin[:, 0::2] *= -1.0
    return cos, sin.astype(np.float32)


def kernel(
    tok_hbm, gains, wq_hbm, wk_hbm, wv_hbm, wo_hbm, cos_hbm, sin_hbm, out_hbm,
    xs, wq, wkv, wo, qb, kvl, kvr, ctx, ctxr, acc, cos, sin, rz, rz0, rr, rr0, rx, rx0, tok,
    s_in, s_send, s_xr, s_xf, s_xe, s_zr, s_sib, s_w, s_kvs, s_kvr, s_ctx, s_rsend, s_rz, s_rr, s_rx, s_out,
):
    tp, dp = lax.axis_index("tp"), lax.axis_index("dp")
    x, zl, c = tp // 4, (tp // 2) % 2, tp % 2
    y, zz = dp // 2, (dp % 2) * 2 + zl

    def device(x_to, z_to, c_to):
        return (x_to * 4 + (z_to % 2) * 2 + c_to, y * 2 + z_to // 2)

    right, left = device((x + 1) % 4, zz, c), device((x + 3) % 4, zz, c)
    above, below = device(x, (zz + 1) % 4, c), device(x, (zz + 3) % 4, c)
    across, sibling = device(x, (zz + 2) % 4, c), device(x, zz, 1 - c)
    b_own, b_right, b_far, b_left = x, (x + 1) % 4, (x + 2) % 4, (x + 3) % 4

    def remote(src, dst, send_sem, recv_sem, to):
        return pltpu.make_async_remote_copy(
            src_ref=src, dst_ref=dst, send_sem=send_sem, recv_sem=recv_sem,
            device_id=to, device_id_type=MESH,
        )

    def sent(ref, sem):
        remote(ref, ref, sem, s_w.at[0], sibling).wait_send()

    def landed(ref, sem):
        remote(ref, ref, s_w.at[0], sem, sibling).wait_recv()

    def cols(q):
        if q is REST_OF_ROW:
            return pl.ds(PIECE, THIRD)
        return pl.ds(pl.multiple_of(q * PIECE, PIECE), PIECE)

    def sem_at(q):
        return 1 if q is REST_OF_ROW else q

    def rows(start, size):
        return pl.ds(pl.multiple_of(start, 32), size)

    tok_copy = pltpu.make_async_copy(tok_hbm, tok, s_in.at[0])
    tok_copy.start()
    barrier = pltpu.get_barrier_semaphore()
    for neighbour in (right, left, above, below, across, sibling):
        pl.semaphore_signal(barrier, inc=1, device_id=neighbour, device_id_type=MESH)

    wk_rows, wv_rows = rows(c * HD, 64), rows(c * HD + 64, 64)
    in_copies = [
        pltpu.make_async_copy(wk_hbm, wkv.at[wk_rows], s_in.at[1]),
        pltpu.make_async_copy(wv_hbm, wkv.at[wv_rows], s_in.at[2]),
        pltpu.make_async_copy(wq_hbm, wq, s_in.at[3]),
        pltpu.make_async_copy(cos_hbm, cos, s_in.at[4]),
        pltpu.make_async_copy(sin_hbm, sin, s_in.at[5]),
        pltpu.make_async_copy(wo_hbm, wo.at[0], s_in.at[6]),
    ]
    for copy in in_copies:
        copy.start()

    tok_copy.wait()

    def norm_rows(i, carry):
        part = pl.ds(pl.multiple_of(i * 16, 16), 16)
        as_float = tok[part, :].astype(F32)
        inv = lax.rsqrt(jnp.mean(as_float * as_float, axis=-1, keepdims=True) + 1e-05)
        normed = scaled(as_float * inv, gains)
        xs[x, pl.ds(pl.multiple_of(c * 64 + i * 16, 16), 16), :] = normed.astype(BF16)
        return carry

    lax.fori_loop(0, 4, norm_rows, 0)
    pl.semaphore_wait(barrier, 6)

    from_below = 192 - 64 * zl
    from_above = 128 + 64 * zl
    x_ways = (right, left)

    def part_ref(b, q, kind, core):
        if kind == 0:
            return xs.at[b, rows(core * 64, 64), cols(q)]
        at = (from_below, from_above)[kind - 1]
        return xs.at[b, rows(at + core * 32, 32), cols(q)]

    def half_ref(b, q, way):
        return xs.at[b, rows(c * 64 + 32 * way, 32), cols(q)]

    def send_x(b, q, way):
        ref = part_ref(b, q, 0, c)
        remote(ref, ref, s_send.at[way, b], s_xr.at[way, b, q], x_ways[way]).start()

    def send_half(b, q, way):
        ref = half_ref(b, q, way)
        remote(ref, ref, s_send.at[way, b], s_xf.at[q], x_ways[way]).start()

    def send_extra(b, kind, way):
        ref = part_ref(b, 0, kind, c)
        remote(ref, ref, s_send.at[7 + way, b], s_xe.at[kind - 1, b], x_ways[way]).start()

    def send_z(b, q):
        for way in range(2):
            at = (from_above, from_below)[way]
            dst = xs.at[b, rows(at + c * 32, 32), cols(q)]
            to = (above, below)[way]
            remote(half_ref(b, q, way), dst, s_send.at[2 + way, b], s_zr.at[b, sem_at(q)], to).start()

    def send_sib(b, q, kind):
        ref = part_ref(b, q, kind, c)
        remote(ref, ref, s_send.at[4 + kind, b], s_sib.at[b, sem_at(q)], sibling).start()

    def recv_sib(b, q):
        landed(xs.at[b, 0:128, cols(q)], s_sib.at[b, sem_at(q)])

    def pass_z(b, q):
        landed(xs.at[b, 0:64, cols(q)], s_zr.at[b, sem_at(q)])
        send_sib(b, q, 1)
        send_sib(b, q, 2)

    send_z(b_own, 0)
    for q in range(1, NQ):
        send_x(b_own, q, 0)
        send_x(b_own, q, 1)
        if q == 1:
            send_z(b_own, REST_OF_ROW)
            send_sib(b_own, 0, 0)
            send_sib(b_own, REST_OF_ROW, 0)
    in_copies[0].wait()
    in_copies[1].wait()
    wkv_sends = [
        remote(wkv.at[wk_rows], wkv.at[wk_rows], s_w.at[0], s_w.at[3], sibling),
        remote(wkv.at[wv_rows], wkv.at[wv_rows], s_w.at[1], s_w.at[4], sibling),
    ]
    for copy in wkv_sends:
        copy.start()

    def wo_part(k):
        part = rows(k * (512 // WO_PARTS), 512 // WO_PARTS)
        return remote(wo_hbm.at[part], wo.at[1, part], s_w.at[2], s_w.at[5], sibling)

    acc[...] = jnp.zeros_like(acc)
    transposed = (((1,), (1,)), ((), ()))

    def qkv_q(a, b, q):
        held = xs[b, :, cols(q)]
        for n in range(2):
            part = pl.ds(n * 256, 256)
            acc[a, :, part] += jnp.dot(held, wq[cols(q), part], preferred_element_type=F32)

    def qkv_kv(a, b, q):
        acc[a, :, pl.ds(512, 256)] += lax.dot_general(
            xs[b, :, cols(q)], wkv[:, cols(q)], transposed, preferred_element_type=F32
        )

    def qkv(a, b, q):
        qkv_q(a, b, q)
        qkv_kv(a, b, q)

    def table(ref, b):
        at = b * BLK
        far = at + (1 - zl) * 128
        parts = [ref[rows(at + zl * 128, 128), :]]
        for half in (1 - zl, zl):
            for core in range(2):
                parts.append(ref[rows(far + core * 64 + half * 32, 32), :])
        return jnp.concatenate(parts, axis=0)

    def kv_send(b):
        return remote(kvl.at[b, c], kvr.at[b, c], s_kvs.at[0, b], s_kvr.at[0, b], across)

    def kv_pass(b):
        return remote(kvr.at[b, c], kvr.at[b, c], s_kvs.at[1, b], s_kvr.at[1, b], sibling)

    def kv_wait(b):
        landed(kvr.at[b, 1 - c], s_kvr.at[1, b])

    def turned(value, b):
        lane = lax.broadcasted_iota(jnp.int32, (BLK, HD), 1)
        swapped = jnp.where(lane % 2 == 0, pltpu.roll(value, HD - 1, 1), pltpu.roll(value, 1, 1))
        return value * table(cos, b) + swapped * table(sin, b)

    def finish_kv(a, b):
        lane = lax.broadcasted_iota(jnp.int32, (BLK, HD), 1)
        first, second = acc[a, :, 512:640], acc[a, :, 640:768]
        key = turned(jnp.where(lane < 64, first, pltpu.roll(second, 64, 1)), b).astype(BF16)
        value = jnp.where(lane < 64, pltpu.roll(first, 64, 1), second).T.astype(BF16)
        for half in range(2):
            kvl[b, half, 0:128] = key[half * 128 : half * 128 + 128]
            kvl[b, half, 128:256] = value[:, half * 128 : half * 128 + 128]
        kv_send(b).start()

    def finish_q(a, b):
        scale = HD**-0.5 * math.log2(math.e)
        for h in range(HEADS):
            head = (turned(acc[a, :, h * HD : (h + 1) * HD], b) * scale).astype(BF16)
            qb[b, h * 192 : h * 192 + 192] = head[0:192]
            qb[b, 768 + h * 64 : 832 + h * 64] = head[192:256]

    def finish_qkv(a, b):
        finish_kv(a, b)
        finish_q(a, b)

    in_copies[2].wait()

    def near_piece(q, carry):
        for b, way in ((b_left, 0), (b_right, 1)):
            landed(part_ref(b, q, 0, c), s_xr.at[way, b, q])
            send_z(b, q)
            send_half(b, q, way)
            send_sib(b, q, 0)
        wo_part(2 * q - 2).start()
        wo_part(2 * q - 1).start()
        return carry

    pass_z(b_own, 0)
    landed(wkv.at[rows((1 - c) * HD, 64)], s_w.at[3])
    landed(wkv.at[rows((1 - c) * HD + 64, 64)], s_w.at[4])
    recv_sib(b_own, 0)
    qkv(2, b_own, 0)
    lax.fori_loop(1, 3, near_piece, 0)
    pass_z(b_own, REST_OF_ROW)
    recv_sib(b_own, REST_OF_ROW)
    qkv(2, b_own, REST_OF_ROW)
    lax.fori_loop(3, 4, near_piece, 0)
    for way in range(2):
        send_x(b_own, 0, way)
    for turn in range(2):
        for way in range(2):
            send_extra(b_own, 1 + (way + turn) % 2, way)
    in_copies[3].wait()
    in_copies[4].wait()
    finish_qkv(2, b_own)
    acc[2] = jnp.zeros((BLK, 768), F32)

    def both(fn):
        def one(a, carry):
            fn(a, (x + 1 + 2 * a) % 4)
            return carry

        lax.fori_loop(0, 2, one, 0)

    def far_rows(q):
        landed(part_ref(b_far, q, 0, c), s_xf.at[q])
        send_sib(b_far, q, 0)

    def far_spread(q):
        far_rows(q)
        send_z(b_far, q)

    def second_loop(i, carry):
        q = i + 1

        @pl.when(i == 1)
        def _():
            far_spread(1)
            far_spread(2)

        @pl.when(i == 2)
        def _():
            far_spread(3)

        for b in (b_left, b_right):
            pass_z(b, q)

        def near(a, b):
            recv_sib(b, q)
            qkv_kv(a, b, q)

        both(near)

        @pl.when(i < 2)
        def _():
            wo_part(6 + i).start()

        return carry

    lax.fori_loop(0, NQ - 1, second_loop, 0)

    def near_first(turn):
        for b, way in ((b_left, 0), (b_right, 1)):
            if turn == 0:
                landed(part_ref(b, 0, 0, c), s_xr.at[way, b, 0])
                send_half(b, 0, way)
                send_sib(b, 0, 0)
            else:
                kind = 1 + (way + turn - 1) % 2
                landed(part_ref(b, 0, kind, c), s_xe.at[kind - 1, b])
                if turn == 1:
                    send_extra(b, kind, way)
                send_sib(b, 0, kind)

    def third_loop(i, carry):
        for kind in range(3):
            pl.when(i == kind)(lambda kind=kind: near_first(kind))
        pass_z(b_far, i + 1)
        recv_sib(b_far, i + 1)
        qkv_kv(2, b_far, i + 1)
        return carry

    lax.fori_loop(0, NQ - 1, third_loop, 0)
    kv_send(b_own).wait_recv()
    kv_pass(b_own).start()

    def near_last(a, b):
        recv_sib(b, 0)
        qkv_kv(a, b, 0)
        finish_kv(a, b)

    near_last(0, b_right)
    far_rows(0)
    near_last(1, b_left)
    for kind in (1, 2):
        landed(part_ref(b_far, 0, kind, c), s_xe.at[kind - 1, b_far])
        send_sib(b_far, 0, kind)
    recv_sib(b_far, 0)
    qkv_kv(2, b_far, 0)
    finish_kv(2, b_far)

    def all_q(a, b):
        def one(q, carry):
            qkv_q(a, b, q)
            return carry

        lax.fori_loop(0, NQ, one, 0)
        finish_q(a, b)


    for b in (b_right, b_left):
        kv_send(b).wait_recv()
        kv_pass(b).start()
    all_q(2, b_far)
    for b in (b_own, b_right, b_left):
        kv_wait(b)

    def place(row):
        other = row >= 192
        inner = jnp.where(other, row - 192, row - 128)
        half = jnp.where(other, zl, 1 - zl)
        far = (1 - zl) * 128 + (inner // 32) * 64 + half * 32 + inner % 32
        return jnp.where(row < 128, zl * 128 + row, far)

    def attend_step(b, kb, state, masked):
        low = lax.broadcasted_iota(jnp.int32, (HD, HD), 1) < 64

        def joined(mine, theirs):
            key = jnp.concatenate([mine[kb, 0, 0:128], mine[kb, 1, 0:64], theirs[kb, 1, 64:128]], axis=0)
            half = jnp.where(low, mine[kb, 1, 128:256].astype(F32), theirs[kb, 1, 128:256].astype(F32))
            return key, jnp.concatenate([mine[kb, 0, 128:256], half.astype(BF16)], axis=1)

        inside, outside = joined(kvl, kvr), joined(kvr, kvl)
        after = []
        for group in range(0, NCH, NCH // 2):
            part = range(group, group + NCH // 2)
            sides = {j: inside if j * CHUNK < 768 else outside for j in part}
            scores = {
                j: lax.dot_general(
                    sides[j][0], qb[b, pl.ds(j * CHUNK, CHUNK)], transposed, preferred_element_type=F32
                )
                for j in part
            }
            if masked:
                column = lax.broadcasted_iota(jnp.int32, (1, CHUNK), 1)
                row = place(lax.broadcasted_iota(jnp.int32, (BLK, 1), 0))
                for j in part:
                    at = j * CHUNK
                    query = (column + at) % 192 if at < 768 else 192 + (column + at - 768) % 64
                    scores[j] = jnp.where(row <= place(query), scores[j], -1e30)
            tops = {
                j: jnp.maximum(state[j][0], jnp.max(scores[j], axis=0, keepdims=True)) for j in part
            }
            weights = {j: jnp.exp2(scores[j] - tops[j]) for j in part}
            for j in part:
                fade = jnp.exp2(state[j][0] - tops[j])
                whole = state[j][1] * fade + jnp.sum(weights[j], axis=0, keepdims=True)
                term = jnp.dot(sides[j][1], weights[j].astype(BF16), preferred_element_type=F32)
                after.append((tops[j], whole, state[j][2] * fade + term))
        return tuple(after)

    def attend(b, before_last=None):
        start = tuple(
            (jnp.full((1, CHUNK), -1e30, F32), jnp.zeros((1, CHUNK), F32), jnp.zeros((HD, CHUNK), F32))
            for _ in range(NCH)
        )
        state = lax.fori_loop(0, b, lambda kb, s: attend_step(b, kb, s, False), start)
        if before_last is not None:
            before_last()
        state = attend_step(b, b, state, True)
        out = [(value / whole).T.astype(BF16) for _, whole, value in state]
        inside, outside = jnp.concatenate(out[:6], axis=0), jnp.concatenate(out[6:], axis=0)
        for h in range(HEADS):
            at = pl.ds(h * HD, HD)
            for core in range(2):
                first, second = h * 192 + core * 64, h * 192 + 128 + core * 32
                third = h * 64 + core * 32
                ctx[b, core, 0:64, at] = inside[first : first + 64]
                ctx[b, core, 64:96, at] = inside[second : second + 32]
                ctx[b, core, 96:128, at] = outside[third : third + 32]
        ctx_send(b).start()

    def ctx_send(b):
        return remote(ctx.at[b, 1 - c], ctxr.at[b], s_ctx.at[0, b], s_ctx.at[1, b], sibling)

    def far_kv():
        kv_send(b_far).wait_recv()
        kv_pass(b_far).start()
        kv_wait(b_far)

    def third_cols(q):
        return pl.ds(pl.multiple_of((q - 1) * REST, REST), REST)

    def sum_cols(q):
        if isinstance(q, int) and q == 0:
            return pl.ds(0, FIRST)
        return pl.ds(pl.multiple_of(FIRST + (q - 1) * REST, 256), REST)

    def project(b, q):
        at = sum_cols(q)
        term = jnp.dot(ctx[b, c], wo[0, :, at], preferred_element_type=F32)
        term += jnp.dot(ctxr[b], wo[1, :, at], preferred_element_type=F32)
        xs[b, 0:128, at] = term.astype(BF16)

    def rs_z(b, q):
        for way in range(2):
            at = (64 + 32 * zl, 96 - 32 * zl)[way]
            place_in = pl.ds(32 - 32 * way, 32)
            dst = rz0.at[place_in] if isinstance(q, int) else rz.at[b, place_in, third_cols(q)]
            src = xs.at[b, rows(at, 32), sum_cols(q)]
            to = (above, below)[way]
            remote(src, dst, s_rsend.at[way, b], s_rz.at[way, b, q], to).start()

    def drain(b, kind):
        quarter, third = xs.at[b, 0:32], xs.at[b, 0:32, 0:THIRD]
        for way in range(2):
            sent(quarter if kind == "own" else third, s_send.at[2 + way, b])
        for part, ref in enumerate((xs.at[b, 0:64], quarter, quarter)):
            sent(ref, s_send.at[4 + part, b])
        if kind == "own":
            for way in range(2):
                sent(xs.at[b, 0:64], s_send.at[way, b])
                sent(xs.at[b, 0:64, 0:PIECE], s_send.at[7 + way, b])
        elif kind in (0, 1):
            sent(quarter, s_send.at[kind, b])
            sent(xs.at[b, 0:32, 0:PIECE], s_send.at[7 + kind, b])

    def sum_z(b, q):
        for way in range(2):
            landed(rz.at[b, pl.ds(32 - 32 * way, 32), third_cols(q)], s_rz.at[way, b, q])
        return xs[b, 0:64, sum_cols(q)].astype(F32) + rz[b, :, third_cols(q)].astype(F32)

    def relay(q, way):
        part = pl.ds(32 * way, 32)
        to = x_ways[way]
        src, dst = xs.at[b_far, part, sum_cols(q)], rr.at[way, :, sum_cols(q)]
        remote(src, dst, s_rsend.at[2 + way, b_far], s_rr.at[way, q], to).start()
        if isinstance(q, int):
            src = xs.at[b_far, pl.ds(64 + 32 * way, 32), sum_cols(0)]
            remote(src, rr0.at[way], s_rsend.at[4 + way, b_far], s_rr.at[way, NQ], to).start()

    def far_sum(q):
        xs[b_far, 0:64, sum_cols(q)] = sum_z(b_far, q).astype(BF16)
        relay(q, 0)
        relay(q, 1)

    def near_sum_first(way):
        b, to = (b_right, b_left)[way], x_ways[way]
        landed(rr.at[way, :, sum_cols(0)], s_rr.at[way, 0])
        landed(rr0.at[way], s_rr.at[way, NQ])
        for at, term in ((32 * way, rr[way, :, sum_cols(0)]), (64 + 32 * way, rr0[way])):
            total = xs[b, at : at + 32, sum_cols(0)].astype(F32) + term.astype(F32)
            xs[b, at : at + 32, sum_cols(0)] = total.astype(BF16)
        src = xs.at[b, 0:128, sum_cols(0)]
        remote(src, rx0.at[way], s_rsend.at[4 + way, b], s_rx.at[way, 0], to).start()

    def near_sum(q, way):
        b, to = (b_right, b_left)[way], x_ways[way]
        landed(rr.at[way, :, sum_cols(q)], s_rr.at[way, q])
        total = sum_z(b, q)
        term = rr[way, :, sum_cols(q)].astype(F32)
        first, second = total[0:32], total[32:64]
        if way == 0:
            first = first + term
        else:
            second = second + term
        xs[b, 0:32, sum_cols(q)] = first.astype(BF16)
        xs[b, 32:64, sum_cols(q)] = second.astype(BF16)
        dst = rx.at[way, :, third_cols(q)]
        remote(xs.at[b, 0:64, sum_cols(q)], dst, s_rsend.at[2 + way, b], s_rx.at[way, q], to).start()

    attend(b_far, far_kv)
    drain(b_far, "far")
    in_copies[5].wait()
    landed(wo.at[1], s_w.at[5])
    ctx_send(b_far).wait_recv()
    project(b_far, 0)
    relay(0, 0)
    relay(0, 1)

    def far_project(i, carry):
        project(b_far, i + 1)
        rs_z(b_far, i + 1)
        return carry

    lax.fori_loop(0, NQ - 1, far_project, 0)
    drain(b_right, 1)
    drain(b_left, 0)

    def near_project(a, b):
        def sums(q, carry):
            far_sum(q)
            return carry

        all_q(a, b)
        lax.fori_loop(3, 3 + a, sums, 0)
        attend(b)
        lax.fori_loop(1, 2 - a, sums, 0)
        ctx_send(b).wait_recv()

        def piece(q, carry):
            project(b, q)
            rs_z(b, q)
            return carry

        lax.fori_loop(1, 2, piece, 0)
        project(b, 0)
        for way in range(2):
            pl.when(a == way)(lambda way=way: near_sum_first(way))
        lax.fori_loop(2, 3 - a, sums, 0)
        lax.fori_loop(2, NQ, piece, 0)

    both(near_project)
    attend(b_own)
    drain(b_own, "own")
    ctx_send(b_own).wait_recv()

    def own_project(q, carry):
        project(b_own, q)
        rs_z(b_own, q)
        near_sum(q, 0)
        near_sum(q, 1)
        return carry

    lax.fori_loop(1, NQ, own_project, 0)
    project(b_own, 0)

    landed(rx0.at[0], s_rx.at[0, 0])
    landed(rx0.at[1], s_rx.at[1, 0])
    whole = xs[b_own, 0:128, sum_cols(0)].astype(F32) + rx0[0].astype(F32) + rx0[1].astype(F32)
    xs[b_own, 0:128, sum_cols(0)] = whole.astype(BF16)
    rs_z(b_own, 0)

    def store(q, head_sum):
        at = sum_cols(q)
        tok[:, at] = (tok[:, at].astype(F32) + head_sum).astype(BF16)
        pltpu.make_async_copy(tok.at[:, at], out_hbm.at[:, at], s_out.at[q]).start()

    def last_sum(q):
        total = sum_z(b_own, q)
        for way in range(2):
            landed(rx.at[way, :, third_cols(q)], s_rx.at[way, q])
        total += rx[0, :, third_cols(q)].astype(F32) + rx[1, :, third_cols(q)].astype(F32)
        store(q, total)

    def last_two(i, carry):
        last_sum(i + 1)
        return carry

    lax.fori_loop(0, 2, last_two, 0)
    for way in range(2):
        landed(rz0.at[pl.ds(32 - 32 * way, 32)], s_rz.at[way, b_own, 0])
    store(0, xs[b_own, 0:64, sum_cols(0)].astype(F32) + rz0[...].astype(F32))
    lax.fori_loop(2, 3, last_two, 0)

    for q in range(NQ):
        pltpu.make_async_copy(tok.at[:, sum_cols(q)], out_hbm.at[:, sum_cols(q)], s_out.at[q]).wait()
    for copy in wkv_sends:
        copy.wait_send()
    sent(wo.at[1], s_w.at[2])
    for b in range(NX):
        kv_send(b).wait_send()
        kv_pass(b).wait_send()
        ctx_send(b).wait_send()
    for way in range(2):
        for b in (b_far, b_right, b_left):
            sent(xs.at[b, 0:32, 0 : 3 * REST], s_rsend.at[way, b])
        sent(xs.at[b_own, 0:32], s_rsend.at[way, b_own])
        sent(xs.at[b_far, 0:32], s_rsend.at[2 + way, b_far])
        sent(xs.at[b_far, 0:32, 0:FIRST], s_rsend.at[4 + way, b_far])
        b = (b_right, b_left)[way]
        sent(xs.at[b, 0:64, 0 : 3 * REST], s_rsend.at[2 + way, b])
        sent(xs.at[b, 0:128, 0:FIRST], s_rsend.at[4 + way, b])


def final_norm(stream_in, gain, stream_out, mlp_out):
    stream = stream_in[...]
    stream_out[...] = stream
    as_float = stream.astype(F32)
    inv = lax.rsqrt(jnp.mean(as_float * as_float, axis=-1, keepdims=True) + 1e-05)
    mlp_out[...] = scaled(as_float * inv, gain).astype(BF16)


def sublayer(tokens, gain_attn, w_query, w_key, w_value, w_out, gain_mlp):
    cos, sin = rotary_tables()
    gain_attn, gain_mlp = gain_attn.reshape(D // HD, HD), gain_mlp.reshape(D // HD, HD)
    any_spec = pl.BlockSpec(memory_space=pl.ANY)
    vmem_spec = pl.BlockSpec(memory_space=pltpu.VMEM)
    dma = pltpu.SemaphoreType.DMA
    shape = jax.ShapeDtypeStruct((64, D), BF16)
    stream = pl.pallas_call(
        kernel,
        out_shape=shape,
        in_specs=[any_spec, vmem_spec] + [any_spec] * 6,
        out_specs=any_spec,
        scratch_shapes=[
            pltpu.VMEM((NX, BLK, D), BF16),
            pltpu.VMEM((D, 512), BF16),
            pltpu.VMEM((256, D), BF16),
            pltpu.VMEM((2, 512, D), BF16),
            pltpu.VMEM((NX, HEADS * BLK, HD), BF16),
            pltpu.VMEM((NX, 2, 256, HD), BF16),
            pltpu.VMEM((NX, 2, 256, HD), BF16),
            pltpu.VMEM((NX, 2, 128, 512), BF16),
            pltpu.VMEM((NX, 128, 512), BF16),
            pltpu.VMEM((3, BLK, 768), F32),
            pltpu.VMEM((NX * BLK, HD), F32),
            pltpu.VMEM((NX * BLK, HD), F32),
            pltpu.VMEM((NX, 64, 3 * REST), BF16),
            pltpu.VMEM((64, FIRST), BF16),
            pltpu.VMEM((2, 32, D), BF16),
            pltpu.VMEM((2, 32, FIRST), BF16),
            pltpu.VMEM((2, 64, 3 * REST), BF16),
            pltpu.VMEM((2, 128, FIRST), BF16),
            pltpu.VMEM((64, D), BF16),
            dma((7,)),
            dma((9, NX)),
            dma((2, NX, NQ)),
            dma((NQ,)),
            dma((2, NX)),
            dma((NX, NQ)),
            dma((NX, NQ)),
            dma((6,)),
            dma((2, NX)),
            dma((2, NX)),
            dma((2, NX)),
            dma((6, NX)),
            dma((2, NX, NQ)),
            dma((2, NQ + 1)),
            dma((2, NQ)),
            dma((NQ,)),
        ],
        compiler_params=pltpu.CompilerParams(
            collective_id=0, has_side_effects=True, vmem_limit_bytes=63 * 2**20
        ),
        cost_estimate=pl.CostEstimate(
            flops=24_000_000_000, bytes_accessed=24_000_000, transcendentals=4_000_000
        ),
    )(
        tokens, gain_attn, w_query, w_key.T, w_value.T, w_out, jnp.asarray(cos), jnp.asarray(sin),
    )
    block = pl.BlockSpec((16, D), lambda i: (i, 0))
    return pl.pallas_call(
        final_norm,
        grid=(4,),
        out_shape=(shape, shape),
        in_specs=[block, pl.BlockSpec((D // HD, HD), lambda i: (0, 0))],
        out_specs=(block, block),
        compiler_params=pltpu.CompilerParams(vmem_limit_bytes=8 * 2**20),
        cost_estimate=pl.CostEstimate(flops=3_000_000, bytes_accessed=3_000_000, transcendentals=64),
    )(stream, gain_mlp)


def solution(mesh):
    placed = (
        P(("dp", "tp"), None),
        P(),
        P(None, "tp"),
        P(None, "tp"),
        P(None, "tp"),
        P("tp", None),
        P(),
    )
    return jax.shard_map(
        sublayer,
        mesh=mesh,
        in_specs=placed,
        out_specs=(P(("dp", "tp"), None), P(("dp", "tp"), None)),
        check_vma=False,
    )
```

```python
import math

import jax
import jax.numpy as jnp
import numpy as np
from jax import lax
from jax.experimental import pallas as pl
from jax.experimental.pallas import tpu as pltpu
from jax.sharding import PartitionSpec as P

MESH = pl.DeviceIdType.MESH
BF16 = jnp.bfloat16
F32 = jnp.float32
D = 8192
HD = 128
NX = 4
BLK = 256
PIECE = 2048
NQ = D // PIECE
HEADS = 4
THIRD = D - PIECE
FIRST = 1280
REST = (D - FIRST) // 3
WO_PARTS = 8
REST_OF_ROW = (1, 2, 3)
NCH = 8
CHUNK = HEADS * BLK // NCH


def scaled(value, gain):
    factor = gain[...].astype(F32)
    parts = [value[:, k * HD : (k + 1) * HD] * factor[k : k + 1] for k in range(D // HD)]
    return jnp.concatenate(parts, axis=1)


def rotary_tables():
    inverse = np.exp(np.arange(HD // 2) * (-2.0 * math.log(500000.0) / HD))
    angles = np.arange(NX * BLK)[:, None] * inverse[None, :]
    cos = np.repeat(np.cos(angles), 2, axis=1).astype(np.float32)
    sin = np.repeat(np.sin(angles), 2, axis=1)
    sin[:, 0::2] *= -1.0
    return cos, sin.astype(np.float32)


def kernel(
    tok_hbm, gains, wq_hbm, wk_hbm, wv_hbm, wo_hbm, cos_hbm, sin_hbm, out_hbm,
    xs, wq, wkv, wo, qb, kvl, kvr, ctx, ctxr, acc, cos, sin, rz, rz0, rr, rr0, rx, rx0, tok,
    s_in, s_send, s_xr, s_xf, s_xe, s_zr, s_sib, s_w, s_kvs, s_kvr, s_ctx, s_rsend, s_rz, s_rr, s_rx, s_out,
):
    tp, dp = lax.axis_index("tp"), lax.axis_index("dp")
    x, zl, c = tp // 4, (tp // 2) % 2, tp % 2
    y, zz = dp // 2, (dp % 2) * 2 + zl

    def device(x_to, z_to, c_to):
        return (x_to * 4 + (z_to % 2) * 2 + c_to, y * 2 + z_to // 2)

    right, left = device((x + 1) % 4, zz, c), device((x + 3) % 4, zz, c)
    above, below = device(x, (zz + 1) % 4, c), device(x, (zz + 3) % 4, c)
    across, sibling = device(x, (zz + 2) % 4, c), device(x, zz, 1 - c)
    opposite = device(x, (zz + 2) % 4, 1 - c)
    b_own, b_right, b_far, b_left = x, (x + 1) % 4, (x + 2) % 4, (x + 3) % 4

    def remote(src, dst, send_sem, recv_sem, to):
        return pltpu.make_async_remote_copy(
            src_ref=src, dst_ref=dst, send_sem=send_sem, recv_sem=recv_sem,
            device_id=to, device_id_type=MESH,
        )

    def sent(ref, sem):
        remote(ref, ref, sem, s_w.at[0], sibling).wait_send()

    def landed(ref, sem):
        remote(ref, ref, s_w.at[0], sem, sibling).wait_recv()

    def cols(q):
        if q is REST_OF_ROW:
            return pl.ds(PIECE, THIRD)
        return pl.ds(pl.multiple_of(q * PIECE, PIECE), PIECE)

    def sem_at(q):
        return 1 if q is REST_OF_ROW else q

    def rows(start, size):
        return pl.ds(pl.multiple_of(start, 32), size)

    tok_copy = pltpu.make_async_copy(tok_hbm, tok, s_in.at[0])
    tok_copy.start()
    barrier = pltpu.get_barrier_semaphore()
    for neighbour in (right, left, above, below, across, opposite, sibling):
        pl.semaphore_signal(barrier, inc=1, device_id=neighbour, device_id_type=MESH)

    wk_rows, wv_rows = rows(c * HD, 64), rows(c * HD + 64, 64)
    in_copies = [
        pltpu.make_async_copy(wk_hbm, wkv.at[wk_rows], s_in.at[1]),
        pltpu.make_async_copy(wv_hbm, wkv.at[wv_rows], s_in.at[2]),
        pltpu.make_async_copy(wq_hbm, wq, s_in.at[3]),
        pltpu.make_async_copy(cos_hbm, cos, s_in.at[4]),
        pltpu.make_async_copy(sin_hbm, sin, s_in.at[5]),
        pltpu.make_async_copy(wo_hbm, wo.at[0], s_in.at[6]),
    ]
    for copy in in_copies:
        copy.start()

    tok_copy.wait()

    def norm_rows(i, carry):
        part = pl.ds(pl.multiple_of(i * 16, 16), 16)
        as_float = tok[part, :].astype(F32)
        inv = lax.rsqrt(jnp.mean(as_float * as_float, axis=-1, keepdims=True) + 1e-05)
        normed = scaled(as_float * inv, gains)
        xs[x, pl.ds(pl.multiple_of(c * 64 + i * 16, 16), 16), :] = normed.astype(BF16)
        return carry

    lax.fori_loop(0, 4, norm_rows, 0)
    pl.semaphore_wait(barrier, 7)

    from_below = 192 - 64 * zl
    from_above = 128 + 64 * zl
    x_ways = (right, left)

    def part_ref(b, q, kind, core):
        if kind == 0:
            return xs.at[b, rows(core * 64, 64), cols(q)]
        at = (from_below, from_above)[kind - 1]
        return xs.at[b, rows(at + core * 32, 32), cols(q)]

    def half_ref(b, q, way):
        return xs.at[b, rows(c * 64 + 32 * way, 32), cols(q)]

    def send_x(b, q, way):
        ref = part_ref(b, q, 0, c)
        remote(ref, ref, s_send.at[way, b], s_xr.at[way, b, q], x_ways[way]).start()

    def send_half(b, q, way):
        ref = half_ref(b, q, way)
        remote(ref, ref, s_send.at[way, b], s_xf.at[q], x_ways[way]).start()

    def send_extra(b, kind, way):
        ref = part_ref(b, 0, kind, c)
        remote(ref, ref, s_send.at[7 + way, b], s_xe.at[kind - 1, b], x_ways[way]).start()

    def send_z(b, q):
        for way in range(2):
            at = (from_above, from_below)[way]
            dst = xs.at[b, rows(at + c * 32, 32), cols(q)]
            to = (above, below)[way]
            remote(half_ref(b, q, way), dst, s_send.at[2 + way, b], s_zr.at[b, sem_at(q)], to).start()

    def send_sib(b, q, kind):
        ref = part_ref(b, q, kind, c)
        remote(ref, ref, s_send.at[4 + kind, b], s_sib.at[b, sem_at(q)], sibling).start()

    def recv_sib(b, q):
        landed(xs.at[b, 0:128, cols(q)], s_sib.at[b, sem_at(q)])

    def pass_z(b, q):
        landed(xs.at[b, 0:64, cols(q)], s_zr.at[b, sem_at(q)])
        send_sib(b, q, 1)
        send_sib(b, q, 2)

    send_z(b_own, 0)
    for q in range(1, NQ):
        send_x(b_own, q, 0)
        send_x(b_own, q, 1)
        if q == 1:
            send_z(b_own, REST_OF_ROW)
            send_sib(b_own, 0, 0)
            send_sib(b_own, REST_OF_ROW, 0)
    in_copies[0].wait()
    in_copies[1].wait()
    wkv_sends = [
        remote(wkv.at[wk_rows], wkv.at[wk_rows], s_w.at[0], s_w.at[3], sibling),
        remote(wkv.at[wv_rows], wkv.at[wv_rows], s_w.at[1], s_w.at[4], sibling),
    ]
    for copy in wkv_sends:
        copy.start()

    def wo_part(k):
        part = rows(k * (512 // WO_PARTS), 512 // WO_PARTS)
        return remote(wo_hbm.at[part], wo.at[1, part], s_w.at[2], s_w.at[5], sibling)

    acc[...] = jnp.zeros_like(acc)
    transposed = (((1,), (1,)), ((), ()))

    def qkv_q(a, b, q):
        held = xs[b, :, cols(q)]
        for n in range(2):
            part = pl.ds(n * 256, 256)
            acc[a, :, part] += jnp.dot(held, wq[cols(q), part], preferred_element_type=F32)

    def qkv_kv(a, b, q):
        acc[a, :, pl.ds(512, 256)] += lax.dot_general(
            xs[b, :, cols(q)], wkv[:, cols(q)], transposed, preferred_element_type=F32
        )

    def qkv(a, b, q):
        qkv_q(a, b, q)
        qkv_kv(a, b, q)

    def table(ref, b):
        at = b * BLK
        far = at + (1 - zl) * 128
        parts = [ref[rows(at + zl * 128, 128), :]]
        for half in (1 - zl, zl):
            for core in range(2):
                parts.append(ref[rows(far + core * 64 + half * 32, 32), :])
        return jnp.concatenate(parts, axis=0)

    def kv_send(b):
        return remote(kvl.at[b, c], kvr.at[b, c], s_kvs.at[0, b], s_kvr.at[0, b], across)

    def kv_pass(b):
        return remote(kvr.at[b, c], kvr.at[b, c], s_kvs.at[1, b], s_kvr.at[1, b], sibling)

    def kv_wait(b):
        landed(kvr.at[b, 1 - c], s_kvr.at[1, b])

    def turned(value, b):
        lane = lax.broadcasted_iota(jnp.int32, (BLK, HD), 1)
        swapped = jnp.where(lane % 2 == 0, pltpu.roll(value, HD - 1, 1), pltpu.roll(value, 1, 1))
        return value * table(cos, b) + swapped * table(sin, b)

    def finish_kv(a, b):
        lane = lax.broadcasted_iota(jnp.int32, (BLK, HD), 1)
        first, second = acc[a, :, 512:640], acc[a, :, 640:768]
        key = turned(jnp.where(lane < 64, first, pltpu.roll(second, 64, 1)), b).astype(BF16)
        value = jnp.where(lane < 64, pltpu.roll(first, 64, 1), second).T.astype(BF16)
        for half in range(2):
            kvl[b, half, 0:128] = key[half * 128 : half * 128 + 128]
            kvl[b, half, 128:256] = value[:, half * 128 : half * 128 + 128]
        kv_send(b).start()

    def finish_q(a, b):
        scale = HD**-0.5 * math.log2(math.e)
        for h in range(HEADS):
            head = (turned(acc[a, :, h * HD : (h + 1) * HD], b) * scale).astype(BF16)
            qb[b, h * 192 : h * 192 + 192] = head[0:192]
            qb[b, 768 + h * 64 : 832 + h * 64] = head[192:256]

    def finish_qkv(a, b):
        finish_kv(a, b)
        finish_q(a, b)

    in_copies[2].wait()

    def near_piece(q, carry):
        for b, way in ((b_left, 0), (b_right, 1)):
            landed(part_ref(b, q, 0, c), s_xr.at[way, b, q])
            send_z(b, q)
            send_half(b, q, way)
            send_sib(b, q, 0)
        wo_part(2 * q - 2).start()
        wo_part(2 * q - 1).start()
        return carry

    pass_z(b_own, 0)
    landed(wkv.at[rows((1 - c) * HD, 64)], s_w.at[3])
    landed(wkv.at[rows((1 - c) * HD + 64, 64)], s_w.at[4])
    recv_sib(b_own, 0)
    qkv(2, b_own, 0)
    lax.fori_loop(1, 3, near_piece, 0)
    pass_z(b_own, REST_OF_ROW)
    recv_sib(b_own, REST_OF_ROW)
    qkv(2, b_own, REST_OF_ROW)
    lax.fori_loop(3, 4, near_piece, 0)
    for way in range(2):
        send_x(b_own, 0, way)
    for turn in range(2):
        for way in range(2):
            send_extra(b_own, 1 + (way + turn) % 2, way)
    in_copies[3].wait()
    in_copies[4].wait()
    finish_qkv(2, b_own)
    acc[2] = jnp.zeros((BLK, 768), F32)

    def both(fn):
        def one(a, carry):
            fn(a, (x + 1 + 2 * a) % 4)
            return carry

        lax.fori_loop(0, 2, one, 0)

    def far_rows(q):
        landed(part_ref(b_far, q, 0, c), s_xf.at[q])
        send_sib(b_far, q, 0)

    def far_spread(q):
        far_rows(q)
        send_z(b_far, q)

    def second_loop(i, carry):
        q = i + 1

        @pl.when(i == 1)
        def _():
            far_spread(1)
            far_spread(2)

        @pl.when(i == 2)
        def _():
            far_spread(3)

        for b in (b_left, b_right):
            pass_z(b, q)

        def near(a, b):
            recv_sib(b, q)
            qkv_kv(a, b, q)

        both(near)

        @pl.when(i < 2)
        def _():
            wo_part(6 + i).start()

        return carry

    lax.fori_loop(0, NQ - 1, second_loop, 0)

    def near_first(turn):
        for b, way in ((b_left, 0), (b_right, 1)):
            if turn == 0:
                landed(part_ref(b, 0, 0, c), s_xr.at[way, b, 0])
                send_half(b, 0, way)
                send_sib(b, 0, 0)
            else:
                kind = 1 + (way + turn - 1) % 2
                landed(part_ref(b, 0, kind, c), s_xe.at[kind - 1, b])
                if turn == 1:
                    send_extra(b, kind, way)
                send_sib(b, 0, kind)

    def third_loop(i, carry):
        for kind in range(3):
            pl.when(i == kind)(lambda kind=kind: near_first(kind))
        pass_z(b_far, i + 1)
        recv_sib(b_far, i + 1)
        qkv_kv(2, b_far, i + 1)
        return carry

    lax.fori_loop(0, NQ - 1, third_loop, 0)
    kv_send(b_own).wait_recv()
    kv_pass(b_own).start()

    def near_last(a, b):
        recv_sib(b, 0)
        qkv_kv(a, b, 0)
        finish_kv(a, b)

    near_last(0, b_right)
    far_rows(0)
    near_last(1, b_left)
    for kind in (1, 2):
        landed(part_ref(b_far, 0, kind, c), s_xe.at[kind - 1, b_far])
        send_sib(b_far, 0, kind)
    recv_sib(b_far, 0)
    kv_both = remote(
        kvl.at[b_far, c], kvr.at[b_far, c], s_kvs.at[1, b_far], s_kvr.at[1, b_far], opposite
    )
    qkv_kv(2, b_far, 0)
    finish_kv(2, b_far)
    kv_both.start()

    def all_q(a, b):
        def one(q, carry):
            qkv_q(a, b, q)
            return carry

        lax.fori_loop(0, NQ, one, 0)
        finish_q(a, b)


    for b in (b_right, b_left):
        kv_send(b).wait_recv()
        kv_pass(b).start()
    all_q(2, b_far)
    for b in (b_own, b_right, b_left):
        kv_wait(b)

    def place(row):
        other = row >= 192
        inner = jnp.where(other, row - 192, row - 128)
        half = jnp.where(other, zl, 1 - zl)
        far = (1 - zl) * 128 + (inner // 32) * 64 + half * 32 + inner % 32
        return jnp.where(row < 128, zl * 128 + row, far)

    def attend_step(b, kb, state, masked):
        low = lax.broadcasted_iota(jnp.int32, (HD, HD), 1) < 64

        def joined(mine, theirs):
            key = jnp.concatenate([mine[kb, 0, 0:128], mine[kb, 1, 0:64], theirs[kb, 1, 64:128]], axis=0)
            half = jnp.where(low, mine[kb, 1, 128:256].astype(F32), theirs[kb, 1, 128:256].astype(F32))
            return key, jnp.concatenate([mine[kb, 0, 128:256], half.astype(BF16)], axis=1)

        inside, outside = joined(kvl, kvr), joined(kvr, kvl)
        after = []
        for group in range(0, NCH, NCH // 2):
            part = range(group, group + NCH // 2)
            sides = {j: inside if j * CHUNK < 768 else outside for j in part}
            scores = {
                j: lax.dot_general(
                    sides[j][0], qb[b, pl.ds(j * CHUNK, CHUNK)], transposed, preferred_element_type=F32
                )
                for j in part
            }
            if masked:
                column = lax.broadcasted_iota(jnp.int32, (1, CHUNK), 1)
                row = place(lax.broadcasted_iota(jnp.int32, (BLK, 1), 0))
                for j in part:
                    at = j * CHUNK
                    query = (column + at) % 192 if at < 768 else 192 + (column + at - 768) % 64
                    scores[j] = jnp.where(row <= place(query), scores[j], -1e30)
            tops = {
                j: jnp.maximum(state[j][0], jnp.max(scores[j], axis=0, keepdims=True)) for j in part
            }
            weights = {j: jnp.exp2(scores[j] - tops[j]) for j in part}
            for j in part:
                fade = jnp.exp2(state[j][0] - tops[j])
                whole = state[j][1] * fade + jnp.sum(weights[j], axis=0, keepdims=True)
                term = jnp.dot(sides[j][1], weights[j].astype(BF16), preferred_element_type=F32)
                after.append((tops[j], whole, state[j][2] * fade + term))
        return tuple(after)

    def attend(b, before_last=None):
        start = tuple(
            (jnp.full((1, CHUNK), -1e30, F32), jnp.zeros((1, CHUNK), F32), jnp.zeros((HD, CHUNK), F32))
            for _ in range(NCH)
        )
        state = lax.fori_loop(0, b, lambda kb, s: attend_step(b, kb, s, False), start)
        if before_last is not None:
            before_last()
        state = attend_step(b, b, state, True)
        out = [(value / whole).T.astype(BF16) for _, whole, value in state]
        inside, outside = jnp.concatenate(out[:6], axis=0), jnp.concatenate(out[6:], axis=0)
        for h in range(HEADS):
            at = pl.ds(h * HD, HD)
            for core in range(2):
                first, second = h * 192 + core * 64, h * 192 + 128 + core * 32
                third = h * 64 + core * 32
                ctx[b, core, 0:64, at] = inside[first : first + 64]
                ctx[b, core, 64:96, at] = inside[second : second + 32]
                ctx[b, core, 96:128, at] = outside[third : third + 32]
        ctx_send(b).start()

    def ctx_send(b):
        return remote(ctx.at[b, 1 - c], ctxr.at[b], s_ctx.at[0, b], s_ctx.at[1, b], sibling)

    def far_kv():
        kv_send(b_far).wait_recv()
        kv_wait(b_far)

    def third_cols(q):
        return pl.ds(pl.multiple_of((q - 1) * REST, REST), REST)

    def sum_cols(q):
        if isinstance(q, int) and q == 0:
            return pl.ds(0, FIRST)
        return pl.ds(pl.multiple_of(FIRST + (q - 1) * REST, 256), REST)

    def project(b, q):
        at = sum_cols(q)
        term = jnp.dot(ctx[b, c], wo[0, :, at], preferred_element_type=F32)
        term += jnp.dot(ctxr[b], wo[1, :, at], preferred_element_type=F32)
        xs[b, 0:128, at] = term.astype(BF16)

    def rs_z(b, q):
        for way in range(2):
            at = (64 + 32 * zl, 96 - 32 * zl)[way]
            place_in = pl.ds(32 - 32 * way, 32)
            dst = rz0.at[place_in] if isinstance(q, int) else rz.at[b, place_in, third_cols(q)]
            src = xs.at[b, rows(at, 32), sum_cols(q)]
            to = (above, below)[way]
            remote(src, dst, s_rsend.at[way, b], s_rz.at[way, b, q], to).start()

    def drain(b, kind):
        quarter, third = xs.at[b, 0:32], xs.at[b, 0:32, 0:THIRD]
        for way in range(2):
            sent(quarter if kind == "own" else third, s_send.at[2 + way, b])
        for part, ref in enumerate((xs.at[b, 0:64], quarter, quarter)):
            sent(ref, s_send.at[4 + part, b])
        if kind == "own":
            for way in range(2):
                sent(xs.at[b, 0:64], s_send.at[way, b])
                sent(xs.at[b, 0:64, 0:PIECE], s_send.at[7 + way, b])
        elif kind in (0, 1):
            sent(quarter, s_send.at[kind, b])
            sent(xs.at[b, 0:32, 0:PIECE], s_send.at[7 + kind, b])

    def sum_z(b, q):
        for way in range(2):
            landed(rz.at[b, pl.ds(32 - 32 * way, 32), third_cols(q)], s_rz.at[way, b, q])
        return xs[b, 0:64, sum_cols(q)].astype(F32) + rz[b, :, third_cols(q)].astype(F32)

    def relay(q, way):
        part = pl.ds(32 * way, 32)
        to = x_ways[way]
        src, dst = xs.at[b_far, part, sum_cols(q)], rr.at[way, :, sum_cols(q)]
        remote(src, dst, s_rsend.at[2 + way, b_far], s_rr.at[way, q], to).start()
        if isinstance(q, int):
            src = xs.at[b_far, pl.ds(64 + 32 * way, 32), sum_cols(0)]
            remote(src, rr0.at[way], s_rsend.at[4 + way, b_far], s_rr.at[way, NQ], to).start()

    def far_sum(q):
        xs[b_far, 0:64, sum_cols(q)] = sum_z(b_far, q).astype(BF16)
        relay(q, 0)
        relay(q, 1)

    def near_sum_first(way):
        b, to = (b_right, b_left)[way], x_ways[way]
        landed(rr.at[way, :, sum_cols(0)], s_rr.at[way, 0])
        landed(rr0.at[way], s_rr.at[way, NQ])
        for at, term in ((32 * way, rr[way, :, sum_cols(0)]), (64 + 32 * way, rr0[way])):
            total = xs[b, at : at + 32, sum_cols(0)].astype(F32) + term.astype(F32)
            xs[b, at : at + 32, sum_cols(0)] = total.astype(BF16)
        src = xs.at[b, 0:128, sum_cols(0)]
        remote(src, rx0.at[way], s_rsend.at[4 + way, b], s_rx.at[way, 0], to).start()

    def near_sum(q, way):
        b, to = (b_right, b_left)[way], x_ways[way]
        landed(rr.at[way, :, sum_cols(q)], s_rr.at[way, q])
        total = sum_z(b, q)
        term = rr[way, :, sum_cols(q)].astype(F32)
        first, second = total[0:32], total[32:64]
        if way == 0:
            first = first + term
        else:
            second = second + term
        xs[b, 0:32, sum_cols(q)] = first.astype(BF16)
        xs[b, 32:64, sum_cols(q)] = second.astype(BF16)
        dst = rx.at[way, :, third_cols(q)]
        remote(xs.at[b, 0:64, sum_cols(q)], dst, s_rsend.at[2 + way, b], s_rx.at[way, q], to).start()

    attend(b_far, far_kv)
    drain(b_far, "far")
    in_copies[5].wait()
    landed(wo.at[1], s_w.at[5])
    ctx_send(b_far).wait_recv()
    project(b_far, 0)
    relay(0, 0)
    relay(0, 1)

    def far_project(i, carry):
        project(b_far, i + 1)
        rs_z(b_far, i + 1)
        return carry

    lax.fori_loop(0, NQ - 1, far_project, 0)
    drain(b_right, 1)
    drain(b_left, 0)

    def near_project(a, b):
        def sums(q, carry):
            far_sum(q)
            return carry

        all_q(a, b)
        lax.fori_loop(3, 3 + a, sums, 0)
        attend(b)
        lax.fori_loop(1, 2 - a, sums, 0)
        ctx_send(b).wait_recv()

        def piece(q, carry):
            project(b, q)
            rs_z(b, q)
            return carry

        lax.fori_loop(1, 2, piece, 0)
        project(b, 0)
        for way in range(2):
            pl.when(a == way)(lambda way=way: near_sum_first(way))
        lax.fori_loop(2, 3 - a, sums, 0)
        lax.fori_loop(2, NQ, piece, 0)

    both(near_project)
    attend(b_own)
    drain(b_own, "own")
    ctx_send(b_own).wait_recv()

    def own_project(q, carry):
        project(b_own, q)
        rs_z(b_own, q)
        near_sum(q, 0)
        near_sum(q, 1)
        return carry

    lax.fori_loop(1, NQ, own_project, 0)
    project(b_own, 0)

    landed(rx0.at[0], s_rx.at[0, 0])
    landed(rx0.at[1], s_rx.at[1, 0])
    whole = xs[b_own, 0:128, sum_cols(0)].astype(F32) + rx0[0].astype(F32) + rx0[1].astype(F32)
    xs[b_own, 0:128, sum_cols(0)] = whole.astype(BF16)
    rs_z(b_own, 0)

    def store(q, head_sum):
        at = sum_cols(q)
        tok[:, at] = (tok[:, at].astype(F32) + head_sum).astype(BF16)
        pltpu.make_async_copy(tok.at[:, at], out_hbm.at[:, at], s_out.at[q]).start()

    def last_sum(q):
        total = sum_z(b_own, q)
        for way in range(2):
            landed(rx.at[way, :, third_cols(q)], s_rx.at[way, q])
        total += rx[0, :, third_cols(q)].astype(F32) + rx[1, :, third_cols(q)].astype(F32)
        store(q, total)

    def last_two(i, carry):
        last_sum(i + 1)
        return carry

    lax.fori_loop(0, 2, last_two, 0)
    for way in range(2):
        landed(rz0.at[pl.ds(32 - 32 * way, 32)], s_rz.at[way, b_own, 0])
    store(0, xs[b_own, 0:64, sum_cols(0)].astype(F32) + rz0[...].astype(F32))
    lax.fori_loop(2, 3, last_two, 0)

    for q in range(NQ):
        pltpu.make_async_copy(tok.at[:, sum_cols(q)], out_hbm.at[:, sum_cols(q)], s_out.at[q]).wait()
    for copy in wkv_sends:
        copy.wait_send()
    sent(wo.at[1], s_w.at[2])
    for b in range(NX):
        kv_send(b).wait_send()
        kv_pass(b).wait_send()
        ctx_send(b).wait_send()
    for way in range(2):
        for b in (b_far, b_right, b_left):
            sent(xs.at[b, 0:32, 0 : 3 * REST], s_rsend.at[way, b])
        sent(xs.at[b_own, 0:32], s_rsend.at[way, b_own])
        sent(xs.at[b_far, 0:32], s_rsend.at[2 + way, b_far])
        sent(xs.at[b_far, 0:32, 0:FIRST], s_rsend.at[4 + way, b_far])
        b = (b_right, b_left)[way]
        sent(xs.at[b, 0:64, 0 : 3 * REST], s_rsend.at[2 + way, b])
        sent(xs.at[b, 0:128, 0:FIRST], s_rsend.at[4 + way, b])


def final_norm(stream_in, gain, stream_out, mlp_out):
    stream = stream_in[...]
    stream_out[...] = stream
    as_float = stream.astype(F32)
    inv = lax.rsqrt(jnp.mean(as_float * as_float, axis=-1, keepdims=True) + 1e-05)
    mlp_out[...] = scaled(as_float * inv, gain).astype(BF16)


def sublayer(tokens, gain_attn, w_query, w_key, w_value, w_out, gain_mlp):
    cos, sin = rotary_tables()
    gain_attn, gain_mlp = gain_attn.reshape(D // HD, HD), gain_mlp.reshape(D // HD, HD)
    any_spec = pl.BlockSpec(memory_space=pl.ANY)
    vmem_spec = pl.BlockSpec(memory_space=pltpu.VMEM)
    dma = pltpu.SemaphoreType.DMA
    shape = jax.ShapeDtypeStruct((64, D), BF16)
    stream = pl.pallas_call(
        kernel,
        out_shape=shape,
        in_specs=[any_spec, vmem_spec] + [any_spec] * 6,
        out_specs=any_spec,
        scratch_shapes=[
            pltpu.VMEM((NX, BLK, D), BF16),
            pltpu.VMEM((D, 512), BF16),
            pltpu.VMEM((256, D), BF16),
            pltpu.VMEM((2, 512, D), BF16),
            pltpu.VMEM((NX, HEADS * BLK, HD), BF16),
            pltpu.VMEM((NX, 2, 256, HD), BF16),
            pltpu.VMEM((NX, 2, 256, HD), BF16),
            pltpu.VMEM((NX, 2, 128, 512), BF16),
            pltpu.VMEM((NX, 128, 512), BF16),
            pltpu.VMEM((3, BLK, 768), F32),
            pltpu.VMEM((NX * BLK, HD), F32),
            pltpu.VMEM((NX * BLK, HD), F32),
            pltpu.VMEM((NX, 64, 3 * REST), BF16),
            pltpu.VMEM((64, FIRST), BF16),
            pltpu.VMEM((2, 32, D), BF16),
            pltpu.VMEM((2, 32, FIRST), BF16),
            pltpu.VMEM((2, 64, 3 * REST), BF16),
            pltpu.VMEM((2, 128, FIRST), BF16),
            pltpu.VMEM((64, D), BF16),
            dma((7,)),
            dma((9, NX)),
            dma((2, NX, NQ)),
            dma((NQ,)),
            dma((2, NX)),
            dma((NX, NQ)),
            dma((NX, NQ)),
            dma((6,)),
            dma((2, NX)),
            dma((2, NX)),
            dma((2, NX)),
            dma((6, NX)),
            dma((2, NX, NQ)),
            dma((2, NQ + 1)),
            dma((2, NQ)),
            dma((NQ,)),
        ],
        compiler_params=pltpu.CompilerParams(
            collective_id=0, has_side_effects=True, vmem_limit_bytes=63 * 2**20
        ),
        cost_estimate=pl.CostEstimate(
            flops=24_000_000_000, bytes_accessed=24_000_000, transcendentals=4_000_000
        ),
    )(
        tokens, gain_attn, w_query, w_key.T, w_value.T, w_out, jnp.asarray(cos), jnp.asarray(sin),
    )
    block = pl.BlockSpec((16, D), lambda i: (i, 0))
    return pl.pallas_call(
        final_norm,
        grid=(4,),
        out_shape=(shape, shape),
        in_specs=[block, pl.BlockSpec((D // HD, HD), lambda i: (0, 0))],
        out_specs=(block, block),
        compiler_params=pltpu.CompilerParams(vmem_limit_bytes=8 * 2**20),
        cost_estimate=pl.CostEstimate(flops=3_000_000, bytes_accessed=3_000_000, transcendentals=64),
    )(stream, gain_mlp)


def solution(mesh):
    placed = (
        P(("dp", "tp"), None),
        P(),
        P(None, "tp"),
        P(None, "tp"),
        P(None, "tp"),
        P("tp", None),
        P(),
    )
    return jax.shard_map(
        sublayer,
        mesh=mesh,
        in_specs=placed,
        out_specs=(P(("dp", "tp"), None), P(("dp", "tp"), None)),
        check_vma=False,
    )
```
